128 devices in a mesh: pool: 8 (over z, y_hi), tp: 16 (over x, y_lo, core).
Axes of the slice: x: 4, y: 4 (y_hi: 2, y_lo: 2; y = y_hi * 2 + y_lo), z: 4, core: 2. Of those that a mesh axis runs over, the one named last changes fastest.
Arguments:
- pre_q: bfloat16 [20480, 8192], P(('pool', 'tp')), may hold values from -250 to 250
- pre_kv: bfloat16 [2, 20480, 1024], P(None, ('pool', 'tp')), may hold values from -6 to 6
- arrival_q: bfloat16 [8, 8192], replicated, may hold values from -250 to 250
- owner: int32 [8], replicated, may hold values from 0 to 7, as said below
- cache_kv: bfloat16 [2, 32, 8192, 1024], P(None, 'pool', 'tp'), may hold values from -6 to 6
- lengths: int32 [32], P('pool'), may hold values from 2 to 8192, as said below
- dec_q: bfloat16 [4, 32, 8192], P(None, 'pool'), may hold values from -250 to 250
- new_kv: bfloat16 [2, 4, 32, 1024], P(None, None, 'pool'), may hold values from -6 to 6
Outputs:
- prefill_out: bfloat16 [20480, 8192], P(('pool', 'tp'))
- received: bfloat16 [2, 16, 2560, 1024], P(None, 'pool', 'tp')
- decode_out: bfloat16 [4, 32, 8192], P(None, 'pool', 'tp')
- arrival_out: bfloat16 [16, 8192], P('pool', 'tp')
The draws below stay inside these ranges and needn't reach their ends.
Inputs may be any that keep to these rules, and one draw needn't show every extreme that they name: `owner`: at most two prompts share one decode group, and some decode group takes exactly two. `lengths`: some request has exactly 8192 resident positions.
All inputs are finite; a program needn't handle non-finite values.
Results may differ from the reference program's by a relative error of at most 0.018.
Values may be sent and summed in bfloat16 or wider, within the bound.
No kernel may reach another device: no remote copies, remote signals or barrier semaphores. Data moves between devices by JAX's collectives and lax.ppermute only.
A program may use at most 192 MiB of HBM per device.

```python
import math
import jax
import jax.numpy as jnp
from jax import lax

H = 64
KVH = 8
HD = 128
STEPS = 4
MOST = 2
SPAN = 2560
PTOK = 20480
CTX = 8192
REQS = 32
SLOTS = 16
N_POOL = 8


def span_pairs(key):
    return jax.random.truncated_normal(jax.random.fold_in(key, 11), -6.0, 6.0, (2, PTOK, KVH * HD), jnp.float32)


def cache_front(key):
    return jax.random.truncated_normal(jax.random.fold_in(key, 12), -6.0, 6.0, (2, REQS, 2, KVH * HD), jnp.float32)


def scaled_queries(key, lead):
    base = jax.random.truncated_normal(key, -6.0, 6.0, lead + (H, HD), jnp.float32)
    levels = jax.random.uniform(jax.random.fold_in(key, 21), lead + (H, 1), jnp.float32, 0.0, math.log(32.0))
    return (base * jnp.exp(levels)).reshape(lead + (H * HD,))


def draw_pre_kv(key, part):
    return span_pairs(key).astype(jnp.bfloat16)


def draw_pre_q(key, part):
    key = jax.random.fold_in(key, 3)
    base = scaled_queries(key, (PTOK,))
    return base.astype(jnp.bfloat16)


def draw_arrival_q(key, part):
    key = jax.random.fold_in(key, 4)
    base = scaled_queries(key, (N_POOL,))
    return base.astype(jnp.bfloat16)


def draw_cache_kv(key, part):
    front = cache_front(key)
    key = jax.random.fold_in(key, 5)
    rest = jax.random.truncated_normal(key, -6.0, 6.0, (2, REQS, CTX - 2, KVH * HD), jnp.float32)
    return jnp.concatenate([front, rest], axis=2).astype(jnp.bfloat16)


def draw_dec_q(key, part):
    key = jax.random.fold_in(key, 6)
    base = scaled_queries(key, (STEPS, REQS))
    return base.astype(jnp.bfloat16)


def draw_lengths(key, part):
    key = jax.random.fold_in(key, 7)
    values = jax.random.randint(key, (REQS,), 2, CTX + 1)
    chosen = jax.random.randint(jax.random.fold_in(key, 1), (), 0, REQS)
    return jnp.where(jnp.arange(REQS) == chosen, CTX, values).astype(jnp.int32)


def draw_owner(key, part):
    key = jax.random.fold_in(key, 8)
    shuffled = jax.random.permutation(key, N_POOL).astype(jnp.int32)
    doubled = jax.random.randint(jax.random.fold_in(key, 1), (), 0, N_POOL - 1).astype(jnp.int32)
    doubled = doubled + (doubled >= 1).astype(jnp.int32)
    return jnp.where(shuffled == 1, doubled, shuffled).astype(jnp.int32)


def block_scale(stream_key, extent, shards, least, high):
    gain = 1.0
    for axis_at, shards_of in shards:
        heights = jax.random.uniform(jax.random.fold_in(jax.random.fold_in(stream_key, 6), axis_at), (shards_of,), jnp.float32, least / len(shards), high / len(shards))
        gain = gain * jnp.repeat(jnp.exp(heights), extent[axis_at] // shards_of).reshape((-1,) + (1,) * (len(extent) - 1 - axis_at))
    return gain


def bell_draw(key, shape, scale, most, split=(), kind=jnp.bfloat16):
    factor_of = block_scale(key, shape, split, -0.22, 0.18) if split else 1.0
    drawn = jax.random.normal(key, shape, jnp.float32) * scale * factor_of
    return jnp.minimum(jnp.maximum(drawn, -most), most).astype(kind)


def setup_inputs(seed: int = 0) -> dict:
    arg_keys = jax.random.split(jax.random.key(seed), 9)
    return {
        "pre_q": draw_pre_q(jax.random.fold_in(arg_keys[8], 71), 0),
        "pre_kv": draw_pre_kv(jax.random.fold_in(arg_keys[8], 71), 0),
        "arrival_q": draw_arrival_q(jax.random.fold_in(arg_keys[8], 71), 0),
        "owner": draw_owner(jax.random.fold_in(arg_keys[8], 71), 0),
        "cache_kv": draw_cache_kv(jax.random.fold_in(arg_keys[8], 71), 0),
        "lengths": draw_lengths(jax.random.fold_in(arg_keys[8], 71), 0),
        "dec_q": draw_dec_q(jax.random.fold_in(arg_keys[8], 71), 0),
        "new_kv": bell_draw(arg_keys[7], (2, STEPS, REQS, KVH * HD), 1.0, 6.0, ((2, 8),)),
    }


NEGATIVE = -1e+30

def attend(queries, key_rows, value_rows, visible):
    score_scale = 1.0 / math.sqrt(HD)
    scores = jnp.einsum('qrd,kd->rqk', queries.astype(jnp.float32), key_rows.astype(jnp.float32)) * score_scale
    shown = visible[None]
    peaks = lax.optimization_barrier(jnp.max(jnp.where(shown, scores, NEGATIVE), axis=-1, keepdims=True))
    weights = jnp.where(shown, jnp.exp(scores - peaks), 0.0)
    totals = lax.optimization_barrier(jnp.sum(weights, axis=-1))
    rounded = lax.optimization_barrier(weights.astype(jnp.bfloat16)).astype(jnp.float32)
    mixed = jnp.einsum('rqk,kd->qrd', rounded, value_rows.astype(jnp.float32))
    return mixed / jnp.transpose(totals)[..., None]

def attend_heads(queries, pair_rows, visible):
    rows = queries.shape[0]
    length = pair_rows.shape[1]
    grouped = jnp.transpose(queries.reshape(rows, KVH, H // KVH, HD), (1, 0, 2, 3))
    key_rows = jnp.transpose(pair_rows[0].reshape(length, KVH, HD), (1, 0, 2))
    value_rows = jnp.transpose(pair_rows[1].reshape(length, KVH, HD), (1, 0, 2))

    def one_group(operands):
        return attend(operands[0], operands[1], operands[2], visible)
    result = lax.map(one_group, (grouped, key_rows, value_rows))
    return jnp.transpose(result, (1, 0, 2, 3)).reshape(rows, H * HD)

def reference(pre_q, pre_kv, arrival_q, owner, cache_kv, lengths, dec_q, new_kv):
    pool_count = owner.shape[0]
    block_q = pre_q.reshape(pool_count, SPAN, H * HD)
    block_kv = jnp.transpose(pre_kv.reshape(2, pool_count, SPAN, KVH * HD), (1, 0, 2, 3))
    places = jnp.arange(SPAN)
    causal = places[None, :] <= places[:, None]

    def prefill_block(operands):
        return attend_heads(operands[0], operands[1], causal).astype(jnp.bfloat16)
    prefill_out = lax.map(prefill_block, (block_q, block_kv)).reshape(PTOK, H * HD)
    prompts = jnp.arange(pool_count)
    shared_owner = owner[:, None] == owner[None, :]
    earlier = prompts[None, :] < prompts[:, None]
    owner_rank = lax.optimization_barrier(jnp.sum(jnp.logical_and(shared_owner, earlier).astype(jnp.int32), axis=1))
    slot = (owner * MOST + owner_rank).astype(jnp.int32)
    span_view = pre_kv.reshape(2, pool_count, SPAN, KVH * HD)
    received = jnp.zeros((2, SLOTS, SPAN, KVH * HD), jnp.bfloat16).at[:, slot].set(span_view)
    whole_view = jnp.ones((1, SPAN), dtype=bool)

    def arrival_block(operands):
        return attend_heads(operands[0][None], operands[1], whole_view)[0]
    arrivals = lax.map(arrival_block, (arrival_q, block_kv))
    arrival_out = jnp.zeros((SLOTS, H * HD), jnp.bfloat16).at[slot].set(arrivals.astype(jnp.bfloat16))
    cache_places = jnp.arange(CTX)
    step_ids = jnp.arange(STEPS)
    tail_view = step_ids[None, :] <= step_ids[:, None]

    def decode_request(operands):
        queries, cache_rows, fresh_rows, length = operands
        pair_rows = jnp.concatenate([cache_rows, fresh_rows], axis=1)
        cache_view = jnp.broadcast_to(cache_places[None, :] < length, (STEPS, CTX))
        visible = jnp.concatenate([cache_view, tail_view], axis=1)
        return attend_heads(queries, pair_rows, visible).astype(jnp.bfloat16)
    decoded = lax.map(decode_request, (jnp.transpose(dec_q, (1, 0, 2)), jnp.transpose(cache_kv, (1, 0, 2, 3)), jnp.transpose(new_kv, (2, 0, 1, 3)), lengths))
    decode_out = jnp.transpose(decoded, (1, 0, 2))
    return (prefill_out, received, decode_out, arrival_out)
```

```python
import functools
import math

import jax
import jax.numpy as jnp
import numpy as np
from jax import lax
from jax.experimental import pallas as pl
from jax.experimental.pallas import tpu as pltpu
from jax.sharding import PartitionSpec as P

H = 64
KVH = 8
REP = H // KVH
HD = 128
STEPS = 4
MOST = 2
POOL = 8
TP = 16
HALF = KVH // 2
NEGATIVE = -1e30
FLOOR = -1e29
SCALE2 = math.log2(math.e) / math.sqrt(HD)
LOG2E = math.log2(math.e)
TILE = 512
UNIT = 64
COLS = 256
VMEM_BYTES = 48 * 1024 * 1024


def params(limit=VMEM_BYTES):
    return pltpu.CompilerParams(vmem_limit_bytes=limit)


def dot_nt(a, b):
    return lax.dot_general(a, b, (((1,), (1,)), ((), ())), preferred_element_type=jnp.float32)


def dot_nn(a, b):
    return lax.dot_general(a, b, (((1,), (0,)), ((), ())), preferred_element_type=jnp.float32)


def prep_kv_kernel(info, kv_ref, own_ref, sib_ref):
    core = info[1]
    for g in range(HALF):
        for half, ref in ((core, own_ref), (1 - core, sib_ref)):
            at = pl.multiple_of((half * HALF + g) * HD, HD)
            ref[g] = kv_ref[:, :, pl.ds(at, HD)]


def prep_kv(info, pre_kv):
    _, tokens, width = pre_kv.shape
    half = jax.ShapeDtypeStruct((HALF, 2, tokens, HD), jnp.bfloat16)
    return pl.pallas_call(
        prep_kv_kernel,
        out_shape=(half, half),
        grid_spec=pltpu.PrefetchScalarGridSpec(
            num_scalar_prefetch=1,
            grid=(1,),
            in_specs=[pl.BlockSpec((2, tokens, width), lambda i, s: (0, 0, 0))],
            out_specs=(
                pl.BlockSpec((HALF, 2, tokens, HD), lambda i, s: (0, 0, 0, 0)),
                pl.BlockSpec((HALF, 2, tokens, HD), lambda i, s: (0, 0, 0, 0)),
            ),
        ),
        compiler_params=params(),
        name="prep_kv",
    )(info, pre_kv)


def copy_kernel(info, x_ref, out_ref):
    out_ref[...] = x_ref[...]


def other_half(info, pre_q):
    tokens = pre_q.shape[0]
    return pl.pallas_call(
        copy_kernel,
        out_shape=jax.ShapeDtypeStruct((tokens, HALF * REP * HD), jnp.bfloat16),
        grid_spec=pltpu.PrefetchScalarGridSpec(
            num_scalar_prefetch=1,
            grid=(2,),
            in_specs=[
                pl.BlockSpec((tokens, 2 * REP * HD), lambda g, s: (0, (1 - s[1]) * 2 + g))
            ],
            out_specs=pl.BlockSpec((tokens, 2 * REP * HD), lambda g, s: (0, g)),
        ),
        compiler_params=params(),
        name="other_half",
    )(info, pre_q)


def place_kernel(info, kept_ref, x_ref, out_ref):
    del kept_ref
    out_ref[...] = x_ref[...]


def place(info, out, x):
    tokens, width = x.shape
    return pl.pallas_call(
        place_kernel,
        out_shape=jax.ShapeDtypeStruct(out.shape, out.dtype),
        grid_spec=pltpu.PrefetchScalarGridSpec(
            num_scalar_prefetch=1,
            grid=(5,),
            in_specs=[
                pl.BlockSpec(memory_space=pl.ANY),
                pl.BlockSpec((tokens // 5, width), lambda i, s: (i, 0)),
            ],
            out_specs=pl.BlockSpec((tokens // 5, width), lambda i, s: (i, 1 - s[1])),
        ),
        input_output_aliases={1: 0},
        compiler_params=params(),
        name="place",
    )(info, out, x)


def prefill_kernel(info, pos_ref, qa_ref, qb_ref, *refs, kinds, first, last):
    count = len(kinds)
    parts, refs = refs[:count], refs[count:]
    if not first:
        carry, refs = ((refs[0], refs[1]), (refs[2], refs[3])), refs[4:]
    if last:
        outs, refs = refs[:2], refs[2:]
    else:
        outs, refs = ((refs[0], refs[1]), (refs[2], refs[3])), refs[4:]
    k_all, v_all, v_across, q_all, s_all, top_all = refs[:6]
    g = pl.program_id(0)
    heads = pl.num_programs(0) - 1
    core = info[1]
    tokens = parts[0].shape[3]
    shard = 2 * tokens
    keys = count * shard
    blocks = q_all.shape[1] // COLS
    tiles = [(lo, min(lo + TILE, keys)) for lo in range(0, keys, TILE)]
    valid = [None if kind < 0 else info[kind] == 1 for kind in kinds]

    @pl.when(g < heads)
    def _():
        for i, part in enumerate(parts):
            for k in range(2):
                at = i * shard + k * tokens
                k_all[at : at + tokens, :] = part[k, 0, 0]
                v_all[at : at + tokens, :] = part[k, 0, 1]
        if v_all.shape[0] > keys:
            v_all[keys:, :] = jnp.zeros((v_all.shape[0] - keys, HD), jnp.bfloat16)
        for at in range(0, v_all.shape[0], 128):
            v_across[g % 2, :, at : at + 128] = v_all[at : at + 128, :].T
        for h in range(REP):
            at = h * tokens
            q_all[0, at : at + tokens, :] = qa_ref[:, h * HD : (h + 1) * HD]
            q_all[1, at : at + tokens, :] = qb_ref[:, h * HD : (h + 1) * HD]

    def scores(side, n):
        q = q_all[side, n * COLS : (n + 1) * COLS, :]
        top = None
        for lo, hi in tiles:
            s = dot_nt(k_all[lo:hi, :], q)
            for at in range(lo, hi, UNIT):
                piece = s[at - lo : at - lo + UNIT, :]
                which = at // shard
                if valid[which] is None:
                    key = lax.broadcasted_iota(jnp.int32, piece.shape, 0) + (at - which * shard)
                    key = jnp.where(key < tokens, key + core * tokens, key - core * tokens)
                    seen = key <= pos_ref[side, n : n + 1, :]
                    piece = jnp.where(seen, piece, NEGATIVE)
                s_all[side, n, at : at + UNIT, :] = piece
                part = jnp.max(piece.reshape(UNIT // 8, 8, COLS), axis=0)
                if valid[which] is not None:
                    part = jnp.where(valid[which], part, NEGATIVE)
                top = part if top is None else jnp.maximum(top, part)
            yield
        top_all[side, n] = top

    def finish(side, n, slot):
        peak = jnp.max(top_all[side, n], axis=0, keepdims=True)
        if not first:
            acc_in, stat_in = carry[side]
            before = stat_in[0, n, 0:1, :]
            peak = jnp.maximum(before, peak)
            shrink = jnp.exp2((before - peak) * SCALE2)
        total = None
        acc = None
        for lo, hi in tiles:
            rounded = []
            for at in range(lo, hi, UNIT):
                which = at // shard
                base = peak if valid[which] is None else jnp.where(valid[which], peak, -NEGATIVE)
                w = jnp.exp2((s_all[side, n, at : at + UNIT, :] - base) * SCALE2)
                part = jnp.sum(w.reshape(UNIT // 8, 8, COLS), axis=0)
                total = part if total is None else total + part
                rounded.append(w.astype(jnp.bfloat16))
            w = jnp.concatenate(rounded, axis=0)
            part = dot_nn(v_across[slot, :, lo:hi], w)
            acc = part if acc is None else acc + part
            yield
        total = jnp.sum(total, axis=0, keepdims=True)
        if not first:
            acc = acc + acc_in[0, n] * shrink
            total = total + stat_in[0, n, 1:2, :] * shrink
        if last:
            stage = refs[6]
            stage[side, n * COLS : (n + 1) * COLS, :] = (acc / total).T.astype(jnp.bfloat16)
        else:
            acc_out, stat_out = outs[side]
            acc_out[0, n] = acc
            line = lax.broadcasted_iota(jnp.int32, (8, COLS), 0)
            stat_out[0, n] = jnp.where(line == 0, peak, total)

    def drain(steps):
        live = list(steps)
        while live:
            for step in list(live):
                if next(step, live) is live:
                    live.remove(step)

    def both(scored, finished, slot):
        steps = []
        for n in range(blocks):
            if scored is not None:
                steps.append(scores(scored, n))
            if finished is not None:
                steps.append(finish(finished, n, slot))
        drain(steps)
        if last and finished is not None:
            stage = refs[6]
            for h in range(REP):
                at = h * tokens
                outs[finished][:, h * HD : (h + 1) * HD] = stage[finished, at : at + tokens, :]

    before = (g + 1) % 2
    pl.when(g == 0)(lambda: both(0, None, None))
    pl.when(jnp.logical_and(g > 0, g < heads))(lambda: both(0, 1, before))
    pl.when(g == heads)(lambda: both(None, 1, before))
    pl.when(g < heads)(lambda: both(1, 0, g % 2))


def prefill(info, pos, pre_q, q_sib, parts, kinds, carry, last):
    tokens = pre_q.shape[0]
    rows = REP * tokens
    blocks = rows // COLS
    first = carry is None
    keys = len(parts) * 2 * tokens
    room = -(-keys // 128) * 128

    def now(g):
        return jnp.minimum(g, HALF - 1)

    def late(g):
        return jnp.maximum(g - 1, 0)

    in_specs = [
        pl.BlockSpec(pos.shape, lambda g, s: (0, 0, 0)),
        pl.BlockSpec((tokens, REP * HD), lambda g, s: (0, s[1] * HALF + now(g))),
        pl.BlockSpec((tokens, REP * HD), lambda g, s: (0, now(g))),
    ]
    in_specs += [
        pl.BlockSpec((2, 1, 2, tokens, HD), lambda g, s: (0, now(g), 0, 0, 0)) for _ in parts
    ]
    args = [pos, pre_q, q_sib, *parts]
    carry_specs = [
        pl.BlockSpec((1, blocks, HD, COLS), lambda g, s: (now(g), 0, 0, 0)),
        pl.BlockSpec((1, blocks, 8, COLS), lambda g, s: (now(g), 0, 0, 0)),
        pl.BlockSpec((1, blocks, HD, COLS), lambda g, s: (late(g), 0, 0, 0)),
        pl.BlockSpec((1, blocks, 8, COLS), lambda g, s: (late(g), 0, 0, 0)),
    ]
    if not first:
        in_specs += carry_specs
        args += list(carry)
    scratch = [
        pltpu.VMEM((keys, HD), jnp.bfloat16),
        pltpu.VMEM((room, HD), jnp.bfloat16),
        pltpu.VMEM((2, HD, room), jnp.bfloat16),
        pltpu.VMEM((2, rows, HD), jnp.bfloat16),
        pltpu.VMEM((2, blocks, keys, COLS), jnp.float32),
        pltpu.VMEM((2, blocks, 8, COLS), jnp.float32),
    ]
    if last:
        out_shape = [
            jax.ShapeDtypeStruct(pre_q.shape, jnp.bfloat16),
            jax.ShapeDtypeStruct(q_sib.shape, jnp.bfloat16),
        ]
        out_specs = [
            pl.BlockSpec((tokens, REP * HD), lambda g, s: (0, s[1] * HALF + now(g))),
            pl.BlockSpec((tokens, REP * HD), lambda g, s: (0, late(g))),
        ]
        scratch.append(pltpu.VMEM((2, rows, HD), jnp.bfloat16))
    else:
        out_shape = [
            jax.ShapeDtypeStruct((HALF, blocks, HD, COLS), jnp.float32),
            jax.ShapeDtypeStruct((HALF, blocks, 8, COLS), jnp.float32),
        ] * 2
        out_specs = carry_specs
    return pl.pallas_call(
        functools.partial(prefill_kernel, kinds=kinds, first=first, last=last),
        out_shape=out_shape,
        grid_spec=pltpu.PrefetchScalarGridSpec(
            num_scalar_prefetch=1,
            grid=(HALF + 1,),
            in_specs=in_specs,
            out_specs=out_specs,
            scratch_shapes=scratch,
        ),
        compiler_params=params(),
        cost_estimate=pl.CostEstimate(
            flops=16 * HALF * rows * keys * HD,
            bytes_accessed=24 * HALF * rows * HD,
            transcendentals=2 * HALF * rows * keys,
        ),
        name="prefill",
    )(info, *args)


def partial_kernel(info, lens, q_ref, aq_ref, cache_ref, tail_ref, pre_ref, out_ref, lse_ref):
    me = info[0]
    r = pl.program_id(0)
    positions = cache_ref.shape[2]
    fresh = tail_ref.shape[2]
    rows = q_ref.shape[2]
    half = rows // 2
    lane = lax.broadcasted_iota(jnp.int32, (half, 128), 1)

    def store(g, slot, peak, total, summed):
        live = total > 0.0
        safe = jnp.where(live, total, 1.0)
        mean = (summed / safe).astype(jnp.bfloat16)
        lse = jnp.where(live, peak * SCALE2 + jnp.log(safe) * LOG2E, NEGATIVE)
        pick = jnp.logical_and(lane % 8 == slot, lane < 24)
        for k in range(2):
            out_ref[2 * g + k, pl.ds(slot, 1)] = mean[k * half : (k + 1) * half][None]
            lse_ref[2 * g + k] = jnp.where(
                pick, lse[k * half : (k + 1) * half], lse_ref[2 * g + k]
            )

    @pl.when(r == 0)
    def _():
        lse_ref[...] = jnp.zeros_like(lse_ref)
        for g in range(KVH):
            cols = slice(g * HD, (g + 1) * HD)
            s = dot_nt(aq_ref[0, g], pre_ref[0, :, cols])
            peak = jnp.max(s, axis=-1, keepdims=True)
            w = jnp.exp2((s - peak) * SCALE2)
            total = jnp.sum(w, axis=-1, keepdims=True)
            store(g, 4, peak, total, dot_nn(w.astype(jnp.bfloat16), pre_ref[1, :, cols]))

    live_here = lens[r] - me * positions
    shown = lax.broadcasted_iota(jnp.int32, (rows, positions), 1) < live_here
    step = (lax.broadcasted_iota(jnp.int32, (rows, fresh), 0) % half) // (half // STEPS)
    at = lax.broadcasted_iota(jnp.int32, (rows, fresh), 1)
    tail_shown = jnp.logical_and(at <= step, me == 0)
    heads = [slice(g * HD, (g + 1) * HD) for g in range(KVH)]
    old = [dot_nt(q_ref[0, g], cache_ref[0, 0, :, cols]) for g, cols in enumerate(heads)]
    new = [dot_nt(q_ref[0, g], tail_ref[0, 0, :, cols]) for g, cols in enumerate(heads)]
    old = [jnp.where(shown, s, NEGATIVE) for s in old]
    new = [jnp.where(tail_shown, t, NEGATIVE) for t in new]
    peaks = [
        jnp.maximum(jnp.max(s, axis=-1, keepdims=True), jnp.max(t, axis=-1, keepdims=True))
        for s, t in zip(old, new)
    ]
    peaks = [jnp.maximum(peak, FLOOR) for peak in peaks]
    old = [jnp.exp2((s - peak) * SCALE2) for s, peak in zip(old, peaks)]
    new = [jnp.exp2((t - peak) * SCALE2) for t, peak in zip(new, peaks)]
    totals = [
        jnp.sum(w, axis=-1, keepdims=True) + jnp.sum(u, axis=-1, keepdims=True)
        for w, u in zip(old, new)
    ]
    old = [w.astype(jnp.bfloat16) for w in old]
    new = [u.astype(jnp.bfloat16) for u in new]
    sums = [
        dot_nn(old[g], cache_ref[1, 0, :, cols]) + dot_nn(new[g], tail_ref[1, 0, :, cols])
        for g, cols in enumerate(heads)
    ]
    for g in range(KVH):
        store(g, r, peaks[g], totals[g], sums[g])

    @pl.when(r == pl.num_programs(0) - 1)
    def _():
        x = lse_ref[...]
        high = x.astype(jnp.bfloat16)
        rest = x - high.astype(jnp.float32)
        mid = rest.astype(jnp.bfloat16)
        low = (rest - mid.astype(jnp.float32)).astype(jnp.bfloat16)
        at = lax.broadcasted_iota(jnp.int32, x.shape, 2)
        parts = jnp.where(
            at < 8,
            high.astype(jnp.float32),
            jnp.where(at < 16, mid.astype(jnp.float32), low.astype(jnp.float32)),
        )
        out_ref[:, 5] = parts.astype(jnp.bfloat16)


def partials(info, lengths, q, arrival, cache_kv, tail, pre_kv):
    requests = lengths.shape[0]
    positions = cache_kv.shape[2]
    tokens = pre_kv.shape[1]
    fresh = tail.shape[2]
    rows = q.shape[2]
    half = rows // 2
    return pl.pallas_call(
        partial_kernel,
        out_shape=jax.ShapeDtypeStruct((TP, requests + 2, half, HD), jnp.bfloat16),
        grid_spec=pltpu.PrefetchScalarGridSpec(
            num_scalar_prefetch=2,
            grid=(requests,),
            in_specs=[
                pl.BlockSpec((1, KVH, rows, HD), lambda r, *_: (r, 0, 0, 0)),
                pl.BlockSpec((1, KVH, rows, HD), lambda r, *_: (0, 0, 0, 0)),
                pl.BlockSpec((2, 1, positions, KVH * HD), lambda r, *_: (0, r, 0, 0)),
                pl.BlockSpec((2, 1, fresh, KVH * HD), lambda r, *_: (0, r, 0, 0)),
                pl.BlockSpec((2, tokens, KVH * HD), lambda r, *_: (0, 0, 0)),
            ],
            out_specs=pl.BlockSpec((TP, requests + 2, half, HD), lambda r, *_: (0, 0, 0, 0)),
            scratch_shapes=[pltpu.VMEM((TP, half, 128), jnp.float32)],
        ),
        compiler_params=params(),
        cost_estimate=pl.CostEstimate(
            flops=40 * rows * KVH * positions * HD * requests,
            bytes_accessed=4 * requests * positions * KVH * HD,
            transcendentals=rows * KVH * positions * requests,
        ),
        name="partials",
    )(info, lengths, q, arrival, cache_kv, tail, pre_kv)


def merge_kernel(x_ref, dec_ref, arr_ref):
    lse = x_ref[:, 5].astype(jnp.float32)
    lane = lax.broadcasted_iota(jnp.int32, lse.shape, 2)
    for slot in range(5):
        pick = jnp.logical_and(lane % 8 == slot, lane < 24)
        mine = jnp.sum(jnp.where(pick, lse, 0.0), axis=-1, keepdims=True)
        top = jnp.max(mine, axis=0, keepdims=True)
        w = jnp.exp2(mine - top)
        total = jnp.sum(w, axis=0)
        mixed = jnp.sum(w * x_ref[:, slot].astype(jnp.float32), axis=0) / total
        if slot < 4:
            dec_ref[slot] = mixed.astype(jnp.bfloat16)
        else:
            arr_ref[...] = mixed.astype(jnp.bfloat16)


def merge(x):
    half = x.shape[2]
    return pl.pallas_call(
        merge_kernel,
        out_shape=(
            jax.ShapeDtypeStruct((4, half, HD), jnp.bfloat16),
            jax.ShapeDtypeStruct((half, HD), jnp.bfloat16),
        ),
        name="merge",
    )(x)


def receive_kernel(table, same_ref, other_ref, out_ref):
    m = pl.program_id(0)
    held, there = table[MOST + m] == 1, table[2 * MOST + m] == 1
    block = jnp.where(there, other_ref[0], same_ref[0])
    out_ref[:, 0] = jnp.where(held, block, jnp.zeros_like(block))


def receive(table, same, other):
    _, two, tokens, width = same.shape
    block = pl.BlockSpec((1, two, tokens, width), lambda m, t: (t[m], 0, 0, 0))
    return pl.pallas_call(
        receive_kernel,
        out_shape=jax.ShapeDtypeStruct((two, MOST, tokens, width), jnp.bfloat16),
        grid_spec=pltpu.PrefetchScalarGridSpec(
            num_scalar_prefetch=1,
            grid=(MOST,),
            in_specs=[block, block],
            out_specs=pl.BlockSpec((two, 1, tokens, width), lambda m, t: (0, m, 0, 0)),
        ),
        compiler_params=params(60 * 1024 * 1024),
        name="receive",
    )(table, same, other)


def body(pre_q, pre_kv, arrival_q, owner, cache_kv, lengths, dec_q, new_kv):
    tokens = pre_q.shape[0]
    me = lax.axis_index("tp").astype(jnp.int32)
    pool = lax.axis_index("pool").astype(jnp.int32)
    x, y = me // 4, me // 2 % 2
    flags = [x >= 1, x >= 2, x == 3, y == 1]
    info = jnp.stack([me, me % 2] + [f.astype(jnp.int32) for f in flags])
    back1, back2, wrapped, upper = 2, 3, 4, 5

    def permute(a, pairs):
        return lax.ppermute(a, "tp", pairs)

    swap = [(t, t ^ 1) for t in range(TP)]
    across = [(t, t ^ 2) for t in range(TP)]
    forward = [(t, t + 4) for t in range(12)]
    around = [(t, t + 12) for t in range(4)]

    kv_own, kv_send = prep_kv(info, pre_kv)
    own = jnp.stack([kv_own, permute(kv_send, swap)])
    q_send = other_half(info, pre_q)
    a1 = permute(own, forward)
    b0 = permute(own, across)
    w1 = permute(own, around)
    q_sib = permute(q_send, swap)
    a2 = permute(a1, forward[4:])
    b1 = permute(a1, across[4:])
    w2 = permute(b0, around)
    b2 = permute(b1, forward[4:])
    _, info_late = lax.optimization_barrier((own, info))

    at = np.arange(REP * tokens) % tokens
    sides = jnp.stack([me % 2, 1 - me % 2]) * tokens
    pos = (sides[:, None] + at[None]).astype(jnp.int32).reshape(2, -1, COLS)

    planes = [[z * 2 + k for z in range(POOL // 2)] for k in range(2)]
    other = lax.ppermute(pre_kv, "pool", [(p, p ^ 1) for p in range(POOL)])
    same = lax.all_gather(pre_kv, "pool", axis=0, axis_index_groups=planes)
    other = lax.all_gather(other, "pool", axis=0, axis_index_groups=planes)
    prompts = jnp.arange(owner.shape[0])
    earlier = jnp.logical_and(
        owner[:, None] == owner[None, :], prompts[None, :] < prompts[:, None]
    )
    rank = jnp.sum(earlier.astype(jnp.int32), axis=1)
    taken = jnp.logical_and(
        owner[None, :] == pool, rank[None, :] == jnp.arange(MOST)[:, None]
    ).astype(jnp.int32)
    prompt_of = jnp.sum(taken * prompts, axis=1)
    held = jnp.sum(taken, axis=1)
    table = jnp.concatenate([prompt_of // 2, held, (prompt_of - pool) % 2]).astype(jnp.int32)
    received = receive(table, same, other)

    requests = lengths.shape[0]
    dec_rows = dec_q.reshape(STEPS, requests, KVH, 2, REP // 2, HD)
    dec_rows = jnp.transpose(dec_rows, (1, 2, 3, 0, 4, 5)).reshape(requests, KVH, STEPS * REP, HD)
    arrival = lax.dynamic_index_in_dim(arrival_q, pool, 0, False)
    arrival = arrival.reshape(KVH, 2, 1, REP // 2, HD)
    arrival = jnp.pad(arrival, ((0, 0), (0, 0), (0, STEPS - 1), (0, 0), (0, 0)))
    arrival = arrival.reshape(1, KVH, STEPS * REP, HD)
    tail = jnp.pad(jnp.transpose(new_kv, (0, 2, 1, 3)), ((0, 0), (0, 0), (0, 12), (0, 0)))
    part = partials(info_late, lengths, dec_rows, arrival, cache_kv, tail, pre_kv)
    part, info_first = lax.optimization_barrier((part, info))
    part = lax.all_to_all(part, "tp", 0, 0)
    decoded, arrived = merge(part)
    arrived, info_next = lax.optimization_barrier((arrived, info))
    decode_out = jnp.transpose(
        decoded.reshape(requests, STEPS, REP // 2, HD), (1, 0, 2, 3)
    ).reshape(STEPS, requests, REP // 2 * HD)

    goes = jnp.logical_and(
        owner[pool] == jnp.arange(POOL)[:, None], rank[pool] == jnp.arange(MOST)[None, :]
    )
    row = arrived[: REP // 2].reshape(1, 1, REP // 2 * HD)
    rows = lax.all_to_all(jnp.where(goes[..., None], row, jnp.zeros_like(row)), "pool", 0, 0)
    arrival_out = jnp.sum(rows.astype(jnp.float32), axis=0).astype(jnp.bfloat16)

    def take(order, parts, kinds, carry, last):
        return prefill(order, pos, pre_q, q_sib, parts, kinds, carry, last)

    carry = take(info_first, [own, a1, b0, w1], [-1, back1, upper, wrapped], None, False)
    carry = take(info_next, [a2, b1, w2], [back2, back1, wrapped], carry, False)
    out, out_send = take(info, [b2], [back2], carry, True)
    prefill_out = place(info, out, permute(out_send, swap))
    return (prefill_out, received, decode_out, arrival_out)


def solution(mesh):
    in_specs = (
        P(("pool", "tp"), None),
        P(None, ("pool", "tp"), None),
        P(),
        P(),
        P(None, "pool", "tp", None),
        P("pool"),
        P(None, "pool", None),
        P(None, None, "pool", None),
    )
    out_specs = (
        P(("pool", "tp"), None),
        P(None, "pool", "tp", None),
        P(None, "pool", "tp"),
        P("pool", "tp"),
    )
    return jax.shard_map(body, mesh=mesh, in_specs=in_specs, out_specs=out_specs, check_vma=False)
```

```python
import functools
import math

import jax
import jax.numpy as jnp
import numpy as np
from jax import lax
from jax.experimental import pallas as pl
from jax.experimental.pallas import tpu as pltpu
from jax.sharding import PartitionSpec as P

H = 64
KVH = 8
REP = H // KVH
HD = 128
STEPS = 4
MOST = 2
POOL = 8
TP = 16
HALF = KVH // 2
NEGATIVE = -1e30
FLOOR = -1e29
SCALE2 = math.log2(math.e) / math.sqrt(HD)
LOG2E = math.log2(math.e)
TILE = 512
UNIT = 64
COLS = 256
VMEM_BYTES = 48 * 1024 * 1024


def params(limit=VMEM_BYTES):
    return pltpu.CompilerParams(vmem_limit_bytes=limit)


def dot_nt(a, b):
    return lax.dot_general(a, b, (((1,), (1,)), ((), ())), preferred_element_type=jnp.float32)


def dot_nn(a, b):
    return lax.dot_general(a, b, (((1,), (0,)), ((), ())), preferred_element_type=jnp.float32)


def prep_kv_kernel(info, kv_ref, own_ref, sib_ref, piece_ref):
    core = info[1]
    for g in range(HALF):
        for half, ref in ((core, own_ref), (1 - core, sib_ref)):
            at = pl.multiple_of((half * HALF + g) * HD, HD)
            ref[g] = kv_ref[:, :, pl.ds(at, HD)]
    width = piece_ref.shape[2]
    for i in range(POOL):
        at = i % 4 * width
        piece_ref[i] = kv_ref[i // 4, :, at : at + width]


def prep_kv(info, pre_kv):
    _, tokens, width = pre_kv.shape
    half = jax.ShapeDtypeStruct((HALF, 2, tokens, HD), jnp.bfloat16)
    return pl.pallas_call(
        prep_kv_kernel,
        out_shape=(half, half, jax.ShapeDtypeStruct((POOL, tokens, width // 4), jnp.bfloat16)),
        grid_spec=pltpu.PrefetchScalarGridSpec(
            num_scalar_prefetch=1,
            grid=(1,),
            in_specs=[pl.BlockSpec((2, tokens, width), lambda i, s: (0, 0, 0))],
            out_specs=(
                pl.BlockSpec((HALF, 2, tokens, HD), lambda i, s: (0, 0, 0, 0)),
                pl.BlockSpec((HALF, 2, tokens, HD), lambda i, s: (0, 0, 0, 0)),
                pl.BlockSpec((POOL, tokens, width // 4), lambda i, s: (0, 0, 0)),
            ),
        ),
        compiler_params=params(),
        name="prep_kv",
    )(info, pre_kv)


def copy_kernel(info, x_ref, out_ref):
    out_ref[...] = x_ref[...]


def other_half(info, pre_q):
    tokens = pre_q.shape[0]
    return pl.pallas_call(
        copy_kernel,
        out_shape=jax.ShapeDtypeStruct((tokens, HALF * REP * HD), jnp.bfloat16),
        grid_spec=pltpu.PrefetchScalarGridSpec(
            num_scalar_prefetch=1,
            grid=(2,),
            in_specs=[
                pl.BlockSpec((tokens, 2 * REP * HD), lambda g, s: (0, (1 - s[1]) * 2 + g))
            ],
            out_specs=pl.BlockSpec((tokens, 2 * REP * HD), lambda g, s: (0, g)),
        ),
        compiler_params=params(),
        name="other_half",
    )(info, pre_q)


def place_kernel(info, kept_ref, x_ref, out_ref):
    del kept_ref
    out_ref[...] = x_ref[...]


def place(info, out, x):
    tokens, width = x.shape
    return pl.pallas_call(
        place_kernel,
        out_shape=jax.ShapeDtypeStruct(out.shape, out.dtype),
        grid_spec=pltpu.PrefetchScalarGridSpec(
            num_scalar_prefetch=1,
            grid=(5,),
            in_specs=[
                pl.BlockSpec(memory_space=pl.ANY),
                pl.BlockSpec((tokens // 5, width), lambda i, s: (i, 0)),
            ],
            out_specs=pl.BlockSpec((tokens // 5, width), lambda i, s: (i, 1 - s[1])),
        ),
        input_output_aliases={1: 0},
        compiler_params=params(),
        name="place",
    )(info, out, x)


def prefill_kernel(info, pos_ref, qa_ref, qb_ref, *refs, kinds, first, last):
    count = len(kinds)
    parts, refs = refs[:count], refs[count:]
    if not first:
        carry, refs = ((refs[0], refs[1]), (refs[2], refs[3])), refs[4:]
    if last:
        outs, refs = refs[:2], refs[2:]
    else:
        outs, refs = ((refs[0], refs[1]), (refs[2], refs[3])), refs[4:]
    k_all, v_all, v_across, q_all, s_all, top_all = refs[:6]
    g = pl.program_id(0)
    heads = pl.num_programs(0) - 1
    core = info[1]
    tokens = parts[0].shape[3]
    shard = 2 * tokens
    keys = count * shard
    blocks = q_all.shape[1] // COLS
    tiles = [(lo, min(lo + TILE, keys)) for lo in range(0, keys, TILE)]
    valid = [None if kind < 0 else info[kind] == 1 for kind in kinds]

    def load():
        for h in range(REP):
            at = h * tokens
            q_all[0, at : at + tokens, :] = qa_ref[:, h * HD : (h + 1) * HD]
            q_all[1, at : at + tokens, :] = qb_ref[:, h * HD : (h + 1) * HD]
        for i, part in enumerate(parts):
            for k in range(2):
                at = i * shard + k * tokens
                k_all[at : at + tokens, :] = part[k, 0, 0]
                v_all[at : at + tokens, :] = part[k, 0, 1]
        if v_all.shape[0] > keys:
            v_all[keys:, :] = jnp.zeros((v_all.shape[0] - keys, HD), jnp.bfloat16)
        for at in range(0, v_all.shape[0], 128):
            v_across[g % 2, :, at : at + 128] = v_all[at : at + 128, :].T

    def scores(side, n):
        q = q_all[side, n * COLS : (n + 1) * COLS, :]
        top = None
        for lo, hi in tiles:
            s = dot_nt(k_all[lo:hi, :], q)
            for at in range(lo, hi, UNIT):
                piece = s[at - lo : at - lo + UNIT, :]
                which = at // shard
                if valid[which] is None:
                    key = lax.broadcasted_iota(jnp.int32, piece.shape, 0) + (at - which * shard)
                    key = jnp.where(key < tokens, key + core * tokens, key - core * tokens)
                    seen = key <= pos_ref[side, n : n + 1, :]
                    piece = jnp.where(seen, piece, NEGATIVE)
                s_all[side, n, at : at + UNIT, :] = piece
                part = jnp.max(piece.reshape(UNIT // 8, 8, COLS), axis=0)
                if valid[which] is not None:
                    part = jnp.where(valid[which], part, NEGATIVE)
                top = part if top is None else jnp.maximum(top, part)
            yield
        top_all[side, n] = top

    def finish(side, n, slot):
        peak = jnp.max(top_all[side, n], axis=0, keepdims=True)
        if not first:
            acc_in, stat_in = carry[side]
            before = stat_in[0, n, 0:1, :]
            peak = jnp.maximum(before, peak)
            shrink = jnp.exp2((before - peak) * SCALE2)
        total = None
        acc = None
        for lo, hi in tiles:
            rounded = []
            for at in range(lo, hi, UNIT):
                which = at // shard
                base = peak if valid[which] is None else jnp.where(valid[which], peak, -NEGATIVE)
                w = jnp.exp2((s_all[side, n, at : at + UNIT, :] - base) * SCALE2)
                part = jnp.sum(w.reshape(UNIT // 8, 8, COLS), axis=0)
                total = part if total is None else total + part
                rounded.append(w.astype(jnp.bfloat16))
            w = jnp.concatenate(rounded, axis=0)
            part = dot_nn(v_across[slot, :, lo:hi], w)
            acc = part if acc is None else acc + part
            yield
        total = jnp.sum(total, axis=0, keepdims=True)
        if not first:
            acc = acc + acc_in[0, n] * shrink
            total = total + stat_in[0, n, 1:2, :] * shrink
        if last:
            stage = refs[6]
            stage[side, n * COLS : (n + 1) * COLS, :] = (acc * (1.0 / total)).T.astype(jnp.bfloat16)
        else:
            acc_out, stat_out = outs[side]
            acc_out[0, n] = acc
            line = lax.broadcasted_iota(jnp.int32, (8, COLS), 0)
            stat_out[0, n] = jnp.where(line == 0, peak, total)

    def drain(steps):
        live = list(steps)
        while live:
            for step in list(live):
                if next(step, live) is live:
                    live.remove(step)

    def both(scored, finished, slot):
        steps = []
        if scored == 0:
            load()
        for n in range(blocks):
            if scored is not None:
                steps.append(scores(scored, n))
            if finished is not None:
                steps.append(finish(finished, n, slot))
        drain(steps)
        if last and finished is not None:
            stage = refs[6]
            for h in range(REP):
                at = h * tokens
                outs[finished][:, h * HD : (h + 1) * HD] = stage[finished, at : at + tokens, :]

    before = (g + 1) % 2
    pl.when(g == 0)(lambda: both(0, None, None))
    pl.when(jnp.logical_and(g > 0, g < heads))(lambda: both(0, 1, before))
    pl.when(g == heads)(lambda: both(None, 1, before))
    pl.when(g < heads)(lambda: both(1, 0, g % 2))


def prefill(info, pos, pre_q, q_sib, parts, kinds, carry, last):
    tokens = pre_q.shape[0]
    rows = REP * tokens
    blocks = rows // COLS
    first = carry is None
    keys = len(parts) * 2 * tokens
    room = -(-keys // 128) * 128

    def now(g):
        return jnp.minimum(g, HALF - 1)

    def late(g):
        return jnp.maximum(g - 1, 0)

    in_specs = [
        pl.BlockSpec(pos.shape, lambda g, s: (0, 0, 0)),
        pl.BlockSpec((tokens, REP * HD), lambda g, s: (0, s[1] * HALF + now(g))),
        pl.BlockSpec((tokens, REP * HD), lambda g, s: (0, now(g))),
    ]
    in_specs += [
        pl.BlockSpec((2, 1, 2, tokens, HD), lambda g, s: (0, now(g), 0, 0, 0)) for _ in parts
    ]
    args = [pos, pre_q, q_sib, *parts]
    carry_specs = [
        pl.BlockSpec((1, blocks, HD, COLS), lambda g, s: (now(g), 0, 0, 0)),
        pl.BlockSpec((1, blocks, 8, COLS), lambda g, s: (now(g), 0, 0, 0)),
        pl.BlockSpec((1, blocks, HD, COLS), lambda g, s: (late(g), 0, 0, 0)),
        pl.BlockSpec((1, blocks, 8, COLS), lambda g, s: (late(g), 0, 0, 0)),
    ]
    if not first:
        in_specs += carry_specs
        args += list(carry)
    scratch = [
        pltpu.VMEM((keys, HD), jnp.bfloat16),
        pltpu.VMEM((room, HD), jnp.bfloat16),
        pltpu.VMEM((2, HD, room), jnp.bfloat16),
        pltpu.VMEM((2, rows, HD), jnp.bfloat16),
        pltpu.VMEM((2, blocks, keys, COLS), jnp.float32),
        pltpu.VMEM((2, blocks, 8, COLS), jnp.float32),
    ]
    if last:
        out_shape = [
            jax.ShapeDtypeStruct(pre_q.shape, jnp.bfloat16),
            jax.ShapeDtypeStruct(q_sib.shape, jnp.bfloat16),
        ]
        out_specs = [
            pl.BlockSpec((tokens, REP * HD), lambda g, s: (0, s[1] * HALF + now(g))),
            pl.BlockSpec((tokens, REP * HD), lambda g, s: (0, late(g))),
        ]
        scratch.append(pltpu.VMEM((2, rows, HD), jnp.bfloat16))
    else:
        out_shape = [
            jax.ShapeDtypeStruct((HALF, blocks, HD, COLS), jnp.float32),
            jax.ShapeDtypeStruct((HALF, blocks, 8, COLS), jnp.float32),
        ] * 2
        out_specs = carry_specs
    return pl.pallas_call(
        functools.partial(prefill_kernel, kinds=kinds, first=first, last=last),
        out_shape=out_shape,
        grid_spec=pltpu.PrefetchScalarGridSpec(
            num_scalar_prefetch=1,
            grid=(HALF + 1,),
            in_specs=in_specs,
            out_specs=out_specs,
            scratch_shapes=scratch,
        ),
        compiler_params=params(),
        cost_estimate=pl.CostEstimate(
            flops=16 * HALF * rows * keys * HD,
            bytes_accessed=24 * HALF * rows * HD,
            transcendentals=2 * HALF * rows * keys,
        ),
        name="prefill",
    )(info, *args)


def partial_kernel(
    info, lens, q_ref, aq_ref, cache, tail_ref, pre_ref, out_ref, q_wide, lse_ref, held, sems
):
    me = info[0]
    r = pl.program_id(0)
    requests, _, positions, _ = held.shape
    fresh = tail_ref.shape[2]
    rows = q_ref.shape[2]
    wide = KVH * rows
    half = rows // 2

    chunk = positions // 2

    def copy(i, j, k):
        some = pl.ds(k * chunk, chunk)
        return pltpu.make_async_copy(
            cache.at[j, i, some], held.at[i, j, some], sems.at[i, j, k]
        )

    @pl.when(r == 0)
    def _():
        for i in range(requests):
            for j in range(2):
                for k in range(2):
                    copy(i, j, k).start()
        q_wide[...] = jnp.zeros_like(q_wide)
        lse_ref[...] = jnp.zeros_like(lse_ref)

    def spread(ref):
        lane = lax.broadcasted_iota(jnp.int32, (HD, 128), 1) // rows
        per = 128 // rows
        for i in range(KVH // per):
            turned = ref[0, i * per : (i + 1) * per].reshape(128, HD).T
            for j in range(per):
                g = i * per + j
                q_wide[g * HD : (g + 1) * HD, i * 128 : (i + 1) * 128] = jnp.where(
                    lane == j, turned, jnp.zeros_like(turned)
                )

    def fold(w):
        return w.reshape(w.shape[0] // 8, 8, wide)

    def weigh(s, t, slot):
        peak = jnp.max(jnp.max(fold(s), axis=0), axis=0, keepdims=True)
        if t is not None:
            peak = jnp.maximum(peak, jnp.max(t, axis=0, keepdims=True))
            peak = jnp.maximum(peak, FLOOR)
        s = jnp.exp2((s - peak) * SCALE2)
        total = jnp.sum(jnp.sum(fold(s), axis=0), axis=0, keepdims=True)
        if t is not None:
            t = jnp.exp2((t - peak) * SCALE2)
            total = total + jnp.sum(t, axis=0, keepdims=True)
        live = total > 0.0
        safe = jnp.where(live, total, 1.0)
        lse_ref[pl.ds(slot, 1), :] = jnp.where(
            live, peak * SCALE2 + jnp.log(safe) * LOG2E, NEGATIVE
        )
        share = jnp.where(live, 1.0 / safe, 0.0)
        s = (s * share).astype(jnp.bfloat16)
        return s, None if t is None else t * share

    def store(g, slot, mean):
        mean = mean.astype(jnp.bfloat16)
        for k in range(2):
            out_ref[2 * g + k, pl.ds(slot, 1)] = mean[k * half : (k + 1) * half][None]

    @pl.when(r == 0)
    def _():
        spread(aq_ref)
        tokens = pre_ref.shape[1]
        w, _ = weigh(dot_nn(pre_ref[0], q_wide[...]), None, 4)
        w = jnp.concatenate([w, jnp.zeros((256 - tokens, wide), jnp.bfloat16)], axis=0).T
        for g in range(KVH):
            values = pre_ref[1, :, g * HD : (g + 1) * HD]
            store(g, 4, dot_nn(w[g * rows : (g + 1) * rows, :tokens], values))

    spread(q_ref)
    q = q_wide[...]
    for j in range(2):
        for k in range(2):
            copy(r, j, k).wait()
    shown = lax.broadcasted_iota(jnp.int32, (positions, wide), 0) < lens[r] - me * positions
    s = jnp.where(shown, dot_nn(held[r, 0], q), NEGATIVE)
    step = lax.broadcasted_iota(jnp.int32, (fresh, wide), 1) % half // (half // STEPS)
    at = lax.broadcasted_iota(jnp.int32, (fresh, wide), 0)
    tail_shown = jnp.logical_and(at <= step, me == 0)
    t = jnp.where(tail_shown, dot_nn(tail_ref[0, 0], q), NEGATIVE)
    w, u = weigh(s, t, r)
    w = w.T
    u = jnp.concatenate([u, jnp.zeros((128 - fresh, wide), jnp.float32)], axis=0).T
    u = u.astype(jnp.bfloat16)
    for g in range(KVH):
        cols = slice(g * HD, (g + 1) * HD)
        mine = slice(g * rows, (g + 1) * rows)
        mean = dot_nn(w[mine, :], held[r, 1, :, cols])
        store(g, r, mean + dot_nn(u[mine, :fresh], tail_ref[1, 0, :, cols]))

    @pl.when(r == pl.num_programs(0) - 1)
    def _():
        x = lse_ref[...]
        high = x.astype(jnp.bfloat16).astype(jnp.float32)
        mid = (x - high).astype(jnp.bfloat16).astype(jnp.float32)
        low = x - high - mid
        rest = jnp.zeros((128 - 3 * x.shape[0], wide), jnp.float32)
        lines = jnp.concatenate([high, mid, low, rest], axis=0).T.astype(jnp.bfloat16)
        for d in range(TP):
            out_ref[d, 5] = lines[d * half : (d + 1) * half, :]


def partials(info, lengths, q, arrival, cache_kv, tail, pre_kv):
    requests = lengths.shape[0]
    positions = cache_kv.shape[2]
    tokens = pre_kv.shape[1]
    fresh = tail.shape[2]
    rows = q.shape[2]
    half = rows // 2
    return pl.pallas_call(
        partial_kernel,
        out_shape=jax.ShapeDtypeStruct((TP, requests + 2, half, HD), jnp.bfloat16),
        grid_spec=pltpu.PrefetchScalarGridSpec(
            num_scalar_prefetch=2,
            grid=(requests,),
            in_specs=[
                pl.BlockSpec((1, KVH, rows, HD), lambda r, *_: (r, 0, 0, 0)),
                pl.BlockSpec((1, KVH, rows, HD), lambda r, *_: (0, 0, 0, 0)),
                pl.BlockSpec(memory_space=pl.ANY),
                pl.BlockSpec((2, 1, fresh, KVH * HD), lambda r, *_: (0, r, 0, 0)),
                pl.BlockSpec((2, tokens, KVH * HD), lambda r, *_: (0, 0, 0)),
            ],
            out_specs=pl.BlockSpec((TP, requests + 2, half, HD), lambda r, *_: (0, 0, 0, 0)),
            scratch_shapes=[
                pltpu.VMEM((KVH * HD, KVH * rows), jnp.bfloat16),
                pltpu.VMEM((8, KVH * rows), jnp.float32),
                pltpu.VMEM((requests, 2, positions, KVH * HD), jnp.bfloat16),
                pltpu.SemaphoreType.DMA((requests, 2, 2)),
            ],
        ),
        compiler_params=params(),
        cost_estimate=pl.CostEstimate(
            flops=40 * rows * KVH * positions * HD * requests,
            bytes_accessed=4 * requests * positions * KVH * HD,
            transcendentals=rows * KVH * positions * requests,
        ),
        name="partials",
    )(info, lengths, q, arrival, cache_kv, tail, pre_kv)


def merge_kernel(x_ref, dec_ref, arr_ref):
    lse = x_ref[:, 5].astype(jnp.float32)
    lane = lax.broadcasted_iota(jnp.int32, lse.shape, 2)
    for slot in range(5):
        pick = jnp.logical_and(lane % 8 == slot, lane < 24)
        mine = jnp.sum(jnp.where(pick, lse, 0.0), axis=-1, keepdims=True)
        top = jnp.max(mine, axis=0, keepdims=True)
        w = jnp.exp2(mine - top)
        total = jnp.sum(w, axis=0)
        mixed = jnp.sum(w * x_ref[:, slot].astype(jnp.float32), axis=0) / total
        if slot < 4:
            dec_ref[slot] = mixed.astype(jnp.bfloat16)
        else:
            arr_ref[...] = mixed.astype(jnp.bfloat16)


def merge(x):
    half = x.shape[2]
    return pl.pallas_call(
        merge_kernel,
        out_shape=(
            jax.ShapeDtypeStruct((4, half, HD), jnp.bfloat16),
            jax.ShapeDtypeStruct((half, HD), jnp.bfloat16),
        ),
        name="merge",
    )(x)


def select_kernel(table, x_ref, arr_ref, out_ref):
    tokens = x_ref.shape[1]
    pool = table[2 * POOL * MOST]
    extra = arr_ref.shape[0]
    for d in range(POOL):
        for m in range(MOST):
            prompt = table[d * MOST + m]
            held = table[POOL * MOST + d * MOST + m] == 1
            x = x_ref[pl.ds(prompt, 1)]
            out_ref[d, m, :tokens] = jnp.where(held, x, jnp.zeros_like(x))[0]
            row = jnp.where(
                jnp.logical_and(held, prompt == pool), arr_ref[...], jnp.zeros_like(arr_ref)
            )
            out_ref[d, m, tokens:, :HD] = row
            out_ref[d, m, tokens:, HD:] = jnp.zeros((extra, x.shape[2] - HD), jnp.bfloat16)


def select(table, pieces, arrived):
    _, tokens, width = pieces.shape
    extra = arrived.shape[0]
    return pl.pallas_call(
        select_kernel,
        out_shape=jax.ShapeDtypeStruct((POOL, MOST, tokens + extra, width), jnp.bfloat16),
        in_specs=[
            pl.BlockSpec(memory_space=pltpu.SMEM),
            pl.BlockSpec(memory_space=pltpu.VMEM),
            pl.BlockSpec(memory_space=pltpu.VMEM),
        ],
        out_specs=pl.BlockSpec(memory_space=pltpu.VMEM),
        compiler_params=params(),
        name="select",
    )(table, pieces, arrived)


def settle_kernel(table, x_ref, kv_ref, arr_ref):
    tokens = kv_ref.shape[2]
    width = x_ref.shape[3]
    pool = table[2 * POOL * MOST]
    for m in range(MOST):
        for i in range(POOL):
            at = i % 4 * width
            kv_ref[i // 4, m, :, at : at + width] = x_ref[i, m, :tokens]
        prompt = table[pool * MOST + m]
        arr_ref[m] = x_ref[pl.ds(prompt, 1), m, tokens:, :HD][0]


def settle(table, x):
    _, _, rows, width = x.shape
    tokens = rows - 16
    return pl.pallas_call(
        settle_kernel,
        out_shape=(
            jax.ShapeDtypeStruct((2, MOST, tokens, KVH * HD), jnp.bfloat16),
            jax.ShapeDtypeStruct((MOST, rows - tokens, HD), jnp.bfloat16),
        ),
        in_specs=[
            pl.BlockSpec(memory_space=pltpu.SMEM),
            pl.BlockSpec(memory_space=pltpu.VMEM),
        ],
        out_specs=(
            pl.BlockSpec(memory_space=pltpu.VMEM),
            pl.BlockSpec(memory_space=pltpu.VMEM),
        ),
        compiler_params=params(),
        name="settle",
    )(table, x)


def body(pre_q, pre_kv, arrival_q, owner, cache_kv, lengths, dec_q, new_kv):
    tokens = pre_q.shape[0]
    me = lax.axis_index("tp").astype(jnp.int32)
    pool = lax.axis_index("pool").astype(jnp.int32)
    x, y = me // 4, me // 2 % 2
    flags = [x >= 1, x >= 2, x == 3, y == 1]
    info = jnp.stack([me, me % 2] + [f.astype(jnp.int32) for f in flags])
    back1, back2, wrapped, upper = 2, 3, 4, 5

    def permute(a, pairs):
        return lax.ppermute(a, "tp", pairs)

    swap = [(t, t ^ 1) for t in range(TP)]
    across = [(t, t ^ 2) for t in range(TP)]
    forward = [(t, t + 4) for t in range(12)]
    around = [(t, t + 12) for t in range(4)]

    at = np.arange(REP * tokens) % tokens
    sides = jnp.stack([me % 2, 1 - me % 2]) * tokens
    pos = (sides[:, None] + at[None]).astype(jnp.int32).reshape(2, -1, COLS)

    prompts = jnp.arange(owner.shape[0])
    earlier = jnp.logical_and(
        owner[:, None] == owner[None, :], prompts[None, :] < prompts[:, None]
    )
    rank = jnp.sum(earlier.astype(jnp.int32), axis=1)
    hit = jnp.logical_and(
        owner[None, None, :] == jnp.arange(POOL)[:, None, None],
        rank[None, None, :] == jnp.arange(MOST)[None, :, None],
    )
    held = jnp.any(hit, axis=-1).astype(jnp.int32)
    prompt_of = jnp.sum(hit.astype(jnp.int32) * prompts, axis=-1).astype(jnp.int32)
    table = jnp.concatenate([prompt_of.reshape(-1), held.reshape(-1), pool[None]])

    requests = lengths.shape[0]
    dec_rows = dec_q.reshape(STEPS, requests, KVH, 2, REP // 2, HD)
    dec_rows = jnp.transpose(dec_rows, (1, 2, 3, 0, 4, 5)).reshape(requests, KVH, STEPS * REP, HD)
    arrival = lax.dynamic_index_in_dim(arrival_q, pool, 0, False)
    arrival = arrival.reshape(KVH, 2, 1, REP // 2, HD)
    arrival = jnp.pad(arrival, ((0, 0), (0, 0), (0, STEPS - 1), (0, 0), (0, 0)))
    arrival = arrival.reshape(1, KVH, STEPS * REP, HD)
    tail = jnp.pad(jnp.transpose(new_kv, (0, 2, 1, 3)), ((0, 0), (0, 0), (0, 12), (0, 0)))

    kv_own, kv_send, pieces = prep_kv(info, pre_kv)
    kv_swapped = permute(kv_send, swap)
    pieces = lax.all_to_all(pieces, "pool", 0, 0)
    q_send = other_half(info, pre_q)
    own = jnp.stack([kv_own, kv_swapped])
    own, q_send, info_decode = lax.optimization_barrier((own, q_send, info))

    a1 = permute(own, forward)
    b0 = permute(own, across)
    w1 = permute(own, around)
    q_sib = permute(q_send, swap)
    part = partials(info_decode, lengths, dec_rows, arrival, cache_kv, tail, pre_kv)
    part = lax.all_to_all(part, "tp", 0, 0)
    part, a1, b0, w1, own, q_sib, info = lax.optimization_barrier(
        (part, a1, b0, w1, own, q_sib, info)
    )

    def take(order, parts, kinds, carry, last):
        return prefill(order, pos, pre_q, q_sib, parts, kinds, carry, last)

    a2 = permute(a1, forward[4:])
    b1 = permute(a1, across[4:])
    w2 = permute(b0, around)
    carry = take(info, [own, a1, b0, w1], [-1, back1, upper, wrapped], None, False)
    decoded, arrived = merge(part)
    arrived, pieces, carry, a2, b1, w2, info = lax.optimization_barrier(
        (arrived, pieces, carry, a2, b1, w2, info)
    )

    b2 = permute(b1, forward[4:])
    landed = lax.all_to_all(select(table, pieces, arrived), "pool", 0, 0)
    carry = take(info, [a2, b1, w2], [back2, back1, wrapped], carry, False)
    carry, b2, landed, info = lax.optimization_barrier((carry, b2, landed, info))

    out, out_send = take(info, [b2], [back2], carry, True)
    received, arrival_rows = settle(table, landed)
    prefill_out = place(info, out, permute(out_send, swap))
    arrival_out = arrival_rows[:, : REP // 2].reshape(MOST, REP // 2 * HD)
    decode_out = jnp.transpose(
        decoded.reshape(requests, STEPS, REP // 2, HD), (1, 0, 2, 3)
    ).reshape(STEPS, requests, REP // 2 * HD)
    return (prefill_out, received, decode_out, arrival_out)


def solution(mesh):
    in_specs = (
        P(("pool", "tp"), None),
        P(None, ("pool", "tp"), None),
        P(),
        P(),
        P(None, "pool", "tp", None),
        P("pool"),
        P(None, "pool", None),
        P(None, None, "pool", None),
    )
    out_specs = (
        P(("pool", "tp"), None),
        P(None, "pool", "tp", None),
        P(None, "pool", "tp"),
        P("pool", "tp"),
    )
    return jax.shard_map(body, mesh=mesh, in_specs=in_specs, out_specs=out_specs, check_vma=False)
```

```python
import functools
import math

import jax
import jax.numpy as jnp
import numpy as np
from jax import lax
from jax.experimental import pallas as pl
from jax.experimental.pallas import tpu as pltpu
from jax.sharding import PartitionSpec as P

H = 64
KVH = 8
REP = H // KVH
HD = 128
STEPS = 4
MOST = 2
POOL = 8
TP = 16
HALF = KVH // 2
NEGATIVE = -1e30
FLOOR = -1e29
SCALE2 = math.log2(math.e) / math.sqrt(HD)
LOG2E = math.log2(math.e)
TILE = 512
UNIT = 64
COLS = 256
VMEM_BYTES = 48 * 1024 * 1024


def params(limit=VMEM_BYTES):
    return pltpu.CompilerParams(vmem_limit_bytes=limit)


def dot_nt(a, b):
    return lax.dot_general(a, b, (((1,), (1,)), ((), ())), preferred_element_type=jnp.float32)


def dot_nn(a, b):
    return lax.dot_general(a, b, (((1,), (0,)), ((), ())), preferred_element_type=jnp.float32)


def prep_kv_kernel(info, kv_ref, own_ref, sib_ref, piece_ref):
    core = info[1]
    for g in range(HALF):
        for half, ref in ((core, own_ref), (1 - core, sib_ref)):
            at = pl.multiple_of((half * HALF + g) * HD, HD)
            ref[g] = kv_ref[:, :, pl.ds(at, HD)]
    width = piece_ref.shape[2]
    for i in range(POOL):
        at = i % 4 * width
        piece_ref[i] = kv_ref[i // 4, :, at : at + width]


def prep_kv(info, pre_kv):
    _, tokens, width = pre_kv.shape
    half = jax.ShapeDtypeStruct((HALF, 2, tokens, HD), jnp.bfloat16)
    return pl.pallas_call(
        prep_kv_kernel,
        out_shape=(half, half, jax.ShapeDtypeStruct((POOL, tokens, width // 4), jnp.bfloat16)),
        grid_spec=pltpu.PrefetchScalarGridSpec(
            num_scalar_prefetch=1,
            grid=(1,),
            in_specs=[pl.BlockSpec((2, tokens, width), lambda i, s: (0, 0, 0))],
            out_specs=(
                pl.BlockSpec((HALF, 2, tokens, HD), lambda i, s: (0, 0, 0, 0)),
                pl.BlockSpec((HALF, 2, tokens, HD), lambda i, s: (0, 0, 0, 0)),
                pl.BlockSpec((POOL, tokens, width // 4), lambda i, s: (0, 0, 0)),
            ),
        ),
        compiler_params=params(),
        name="prep_kv",
    )(info, pre_kv)


def copy_kernel(info, x_ref, out_ref):
    out_ref[...] = x_ref[...]


def other_half(info, pre_q):
    tokens = pre_q.shape[0]
    return pl.pallas_call(
        copy_kernel,
        out_shape=jax.ShapeDtypeStruct((tokens, HALF * REP * HD), jnp.bfloat16),
        grid_spec=pltpu.PrefetchScalarGridSpec(
            num_scalar_prefetch=1,
            grid=(2,),
            in_specs=[
                pl.BlockSpec((tokens, 2 * REP * HD), lambda g, s: (0, (1 - s[1]) * 2 + g))
            ],
            out_specs=pl.BlockSpec((tokens, 2 * REP * HD), lambda g, s: (0, g)),
        ),
        compiler_params=params(),
        name="other_half",
    )(info, pre_q)


def place_kernel(info, kept_ref, x_ref, out_ref):
    del kept_ref
    out_ref[...] = x_ref[...]


def place(info, out, x):
    tokens, width = x.shape
    return pl.pallas_call(
        place_kernel,
        out_shape=jax.ShapeDtypeStruct(out.shape, out.dtype),
        grid_spec=pltpu.PrefetchScalarGridSpec(
            num_scalar_prefetch=1,
            grid=(5,),
            in_specs=[
                pl.BlockSpec(memory_space=pl.ANY),
                pl.BlockSpec((tokens // 5, width), lambda i, s: (i, 0)),
            ],
            out_specs=pl.BlockSpec((tokens // 5, width), lambda i, s: (i, 1 - s[1])),
        ),
        input_output_aliases={1: 0},
        compiler_params=params(),
        name="place",
    )(info, out, x)


def prefill_kernel(info, pos_ref, qa_ref, qb_ref, *refs, kinds, first, last):
    count = len(kinds)
    parts, refs = refs[:count], refs[count:]
    if not first:
        carry, refs = ((refs[0], refs[1]), (refs[2], refs[3])), refs[4:]
    if last:
        outs, refs = refs[:2], refs[2:]
    else:
        outs, refs = ((refs[0], refs[1]), (refs[2], refs[3])), refs[4:]
    k_all, v_all, v_across, q_all, s_all, top_all = refs[:6]
    g = pl.program_id(0)
    heads = pl.num_programs(0) - 1
    core = info[1]
    tokens = parts[0].shape[3]
    shard = 2 * tokens
    keys = count * shard
    blocks = q_all.shape[1] // COLS
    tiles = [(lo, min(lo + TILE, keys)) for lo in range(0, keys, TILE)]
    valid = [None if kind < 0 else info[kind] == 1 for kind in kinds]

    def load():
        for h in range(REP):
            at = h * tokens
            q_all[0, at : at + tokens, :] = qa_ref[:, h * HD : (h + 1) * HD]
            q_all[1, at : at + tokens, :] = qb_ref[:, h * HD : (h + 1) * HD]
        for i, part in enumerate(parts):
            for k in range(2):
                at = i * shard + k * tokens
                k_all[at : at + tokens, :] = part[k, 0, 0]
                v_all[at : at + tokens, :] = part[k, 0, 1]
        if v_all.shape[0] > keys:
            v_all[keys:, :] = jnp.zeros((v_all.shape[0] - keys, HD), jnp.bfloat16)
        for at in range(0, v_all.shape[0], 128):
            v_across[g % 2, :, at : at + 128] = v_all[at : at + 128, :].T

    def scores(side, n):
        q = q_all[side, n * COLS : (n + 1) * COLS, :]
        top = None
        for lo, hi in tiles:
            s = dot_nt(k_all[lo:hi, :], q)
            for at in range(lo, hi, UNIT):
                piece = s[at - lo : at - lo + UNIT, :]
                which = at // shard
                if valid[which] is None:
                    key = lax.broadcasted_iota(jnp.int32, piece.shape, 0) + (at - which * shard)
                    key = jnp.where(key < tokens, key + core * tokens, key - core * tokens)
                    seen = key <= pos_ref[side, n : n + 1, :]
                    piece = jnp.where(seen, piece, NEGATIVE)
                s_all[side, n, at : at + UNIT, :] = piece
                part = jnp.max(piece.reshape(UNIT // 8, 8, COLS), axis=0)
                if valid[which] is not None:
                    part = jnp.where(valid[which], part, NEGATIVE)
                top = part if top is None else jnp.maximum(top, part)
            yield
        top_all[side, n] = top

    def finish(side, n, slot):
        peak = jnp.max(top_all[side, n], axis=0, keepdims=True)
        if not first:
            acc_in, stat_in = carry[side]
            before = stat_in[0, n, 0:1, :]
            peak = jnp.maximum(before, peak)
            shrink = jnp.exp2((before - peak) * SCALE2)
        total = None
        acc = None
        for lo, hi in tiles:
            rounded = []
            for at in range(lo, hi, UNIT):
                which = at // shard
                base = peak if valid[which] is None else jnp.where(valid[which], peak, -NEGATIVE)
                w = jnp.exp2((s_all[side, n, at : at + UNIT, :] - base) * SCALE2)
                part = jnp.sum(w.reshape(UNIT // 8, 8, COLS), axis=0)
                total = part if total is None else total + part
                rounded.append(w.astype(jnp.bfloat16))
            w = jnp.concatenate(rounded, axis=0)
            part = dot_nn(v_across[slot, :, lo:hi], w)
            acc = part if acc is None else acc + part
            yield
        total = jnp.sum(total, axis=0, keepdims=True)
        if not first:
            acc = acc + acc_in[0, n].astype(jnp.float32) * shrink
            total = total + stat_in[0, n, 1:2, :] * shrink
        if last:
            stage = refs[6]
            stage[side, n * COLS : (n + 1) * COLS, :] = (acc * (1.0 / total)).T.astype(jnp.bfloat16)
        else:
            acc_out, stat_out = outs[side]
            acc_out[0, n] = acc.astype(jnp.bfloat16)
            line = lax.broadcasted_iota(jnp.int32, (8, COLS), 0)
            stat_out[0, n] = jnp.where(line == 0, peak, total)

    def drain(steps):
        live = list(steps)
        while live:
            for step in list(live):
                if next(step, live) is live:
                    live.remove(step)

    def both(scored, finished, slot):
        if scored == 0:
            load()
        for n in range(blocks):
            steps = [] if scored is None else [scores(scored, n)]
            if finished is not None:
                steps.append(finish(finished, n, slot))
            drain(steps)
        if last and finished is not None:
            stage = refs[6]
            for h in range(REP):
                at = h * tokens
                outs[finished][:, h * HD : (h + 1) * HD] = stage[finished, at : at + tokens, :]

    before = (g + 1) % 2
    pl.when(g == 0)(lambda: both(0, None, None))
    pl.when(jnp.logical_and(g > 0, g < heads))(lambda: both(0, 1, before))
    pl.when(g == heads)(lambda: both(None, 1, before))
    pl.when(g < heads)(lambda: both(1, 0, g % 2))


def prefill(info, pos, pre_q, q_sib, parts, kinds, carry, last):
    tokens = pre_q.shape[0]
    rows = REP * tokens
    blocks = rows // COLS
    first = carry is None
    keys = len(parts) * 2 * tokens
    room = -(-keys // 128) * 128

    def now(g):
        return jnp.minimum(g, HALF - 1)

    def late(g):
        return jnp.maximum(g - 1, 0)

    in_specs = [
        pl.BlockSpec(pos.shape, lambda g, s: (0, 0, 0)),
        pl.BlockSpec((tokens, REP * HD), lambda g, s: (0, s[1] * HALF + now(g))),
        pl.BlockSpec((tokens, REP * HD), lambda g, s: (0, now(g))),
    ]
    in_specs += [
        pl.BlockSpec((2, 1, 2, tokens, HD), lambda g, s: (0, now(g), 0, 0, 0)) for _ in parts
    ]
    args = [pos, pre_q, q_sib, *parts]
    carry_specs = [
        pl.BlockSpec((1, blocks, HD, COLS), lambda g, s: (now(g), 0, 0, 0)),
        pl.BlockSpec((1, blocks, 8, COLS), lambda g, s: (now(g), 0, 0, 0)),
        pl.BlockSpec((1, blocks, HD, COLS), lambda g, s: (late(g), 0, 0, 0)),
        pl.BlockSpec((1, blocks, 8, COLS), lambda g, s: (late(g), 0, 0, 0)),
    ]
    if not first:
        in_specs += carry_specs
        args += list(carry)
    scratch = [
        pltpu.VMEM((keys, HD), jnp.bfloat16),
        pltpu.VMEM((room, HD), jnp.bfloat16),
        pltpu.VMEM((2, HD, room), jnp.bfloat16),
        pltpu.VMEM((2, rows, HD), jnp.bfloat16),
        pltpu.VMEM((2, blocks, keys, COLS), jnp.float32),
        pltpu.VMEM((2, blocks, 8, COLS), jnp.float32),
    ]
    if last:
        out_shape = [
            jax.ShapeDtypeStruct(pre_q.shape, jnp.bfloat16),
            jax.ShapeDtypeStruct(q_sib.shape, jnp.bfloat16),
        ]
        out_specs = [
            pl.BlockSpec((tokens, REP * HD), lambda g, s: (0, s[1] * HALF + now(g))),
            pl.BlockSpec((tokens, REP * HD), lambda g, s: (0, late(g))),
        ]
        scratch.append(pltpu.VMEM((2, rows, HD), jnp.bfloat16))
    else:
        out_shape = [
            jax.ShapeDtypeStruct((HALF, blocks, HD, COLS), jnp.bfloat16),
            jax.ShapeDtypeStruct((HALF, blocks, 8, COLS), jnp.float32),
        ] * 2
        out_specs = carry_specs
    return pl.pallas_call(
        functools.partial(prefill_kernel, kinds=kinds, first=first, last=last),
        out_shape=out_shape,
        grid_spec=pltpu.PrefetchScalarGridSpec(
            num_scalar_prefetch=1,
            grid=(HALF + 1,),
            in_specs=in_specs,
            out_specs=out_specs,
            scratch_shapes=scratch,
        ),
        compiler_params=params(),
        cost_estimate=pl.CostEstimate(
            flops=16 * HALF * rows * keys * HD,
            bytes_accessed=24 * HALF * rows * HD,
            transcendentals=2 * HALF * rows * keys,
        ),
        name="prefill",
    )(info, *args)


def partial_kernel(
    info, lens, q_ref, aq_ref, cache, tail_ref, pre_ref, out_ref, q_wide, lse_ref, held, sems
):
    me = info[0]
    r = pl.program_id(0)
    requests, _, positions, _ = held.shape
    fresh = tail_ref.shape[2]
    rows = q_ref.shape[2]
    wide = KVH * rows
    half = rows // 2

    chunk = positions // 2

    def copy(i, j, k):
        some = pl.ds(k * chunk, chunk)
        return pltpu.make_async_copy(
            cache.at[j, i, some], held.at[i, j, some], sems.at[i, j, k]
        )

    @pl.when(r == 0)
    def _():
        for i in range(requests):
            for j in range(2):
                for k in range(2):
                    copy(i, j, k).start()
        q_wide[...] = jnp.zeros_like(q_wide)
        lse_ref[...] = jnp.zeros_like(lse_ref)

    def spread(ref):
        lane = lax.broadcasted_iota(jnp.int32, (HD, 128), 1) // rows
        per = 128 // rows
        for i in range(KVH // per):
            turned = ref[0, i * per : (i + 1) * per].reshape(128, HD).T
            for j in range(per):
                g = i * per + j
                q_wide[g * HD : (g + 1) * HD, i * 128 : (i + 1) * 128] = jnp.where(
                    lane == j, turned, jnp.zeros_like(turned)
                )

    def fold(w):
        return w.reshape(w.shape[0] // 8, 8, wide)

    def weigh(s, t, slot):
        peak = jnp.max(jnp.max(fold(s), axis=0), axis=0, keepdims=True)
        if t is not None:
            peak = jnp.maximum(peak, jnp.max(t, axis=0, keepdims=True))
            peak = jnp.maximum(peak, FLOOR)
        s = jnp.exp2((s - peak) * SCALE2)
        total = jnp.sum(jnp.sum(fold(s), axis=0), axis=0, keepdims=True)
        if t is not None:
            t = jnp.exp2((t - peak) * SCALE2)
            total = total + jnp.sum(t, axis=0, keepdims=True)
        live = total > 0.0
        safe = jnp.where(live, total, 1.0)
        lse_ref[pl.ds(slot, 1), :] = jnp.where(
            live, peak * SCALE2 + jnp.log(safe) * LOG2E, NEGATIVE
        )
        share = jnp.where(live, 1.0 / safe, 0.0)
        s = (s * share).astype(jnp.bfloat16)
        return s, None if t is None else t * share

    def store(g, slot, mean):
        mean = mean.astype(jnp.bfloat16)
        for k in range(2):
            out_ref[2 * g + k, pl.ds(slot, 1)] = mean[k * half : (k + 1) * half][None]

    @pl.when(r == 0)
    def _():
        spread(aq_ref)
        tokens = pre_ref.shape[1]
        w, _ = weigh(dot_nn(pre_ref[0], q_wide[...]), None, 4)
        w = jnp.concatenate([w, jnp.zeros((256 - tokens, wide), jnp.bfloat16)], axis=0).T
        for g in range(KVH):
            values = pre_ref[1, :, g * HD : (g + 1) * HD]
            store(g, 4, dot_nn(w[g * rows : (g + 1) * rows, :tokens], values))

    spread(q_ref)
    q = q_wide[...]
    for j in range(2):
        for k in range(2):
            copy(r, j, k).wait()
    shown = lax.broadcasted_iota(jnp.int32, (positions, wide), 0) < lens[r] - me * positions
    s = jnp.where(shown, dot_nn(held[r, 0], q), NEGATIVE)
    step = lax.broadcasted_iota(jnp.int32, (fresh, wide), 1) % half // (half // STEPS)
    at = lax.broadcasted_iota(jnp.int32, (fresh, wide), 0)
    tail_shown = jnp.logical_and(at <= step, me == 0)
    t = jnp.where(tail_shown, dot_nn(tail_ref[0, 0], q), NEGATIVE)
    w, u = weigh(s, t, r)
    w = w.T
    u = jnp.concatenate([u, jnp.zeros((128 - fresh, wide), jnp.float32)], axis=0).T
    u = u.astype(jnp.bfloat16)
    for g in range(KVH):
        cols = slice(g * HD, (g + 1) * HD)
        mine = slice(g * rows, (g + 1) * rows)
        mean = dot_nn(w[mine, :], held[r, 1, :, cols])
        store(g, r, mean + dot_nn(u[mine, :fresh], tail_ref[1, 0, :, cols]))

    @pl.when(r == pl.num_programs(0) - 1)
    def _():
        x = lse_ref[...]
        high = x.astype(jnp.bfloat16).astype(jnp.float32)
        mid = (x - high).astype(jnp.bfloat16).astype(jnp.float32)
        low = x - high - mid
        rest = jnp.zeros((128 - 3 * x.shape[0], wide), jnp.float32)
        lines = jnp.concatenate([high, mid, low, rest], axis=0).T.astype(jnp.bfloat16)
        for d in range(TP):
            out_ref[d, 5] = lines[d * half : (d + 1) * half, :]


def partials(info, lengths, q, arrival, cache_kv, tail, pre_kv):
    requests = lengths.shape[0]
    positions = cache_kv.shape[2]
    tokens = pre_kv.shape[1]
    fresh = tail.shape[2]
    rows = q.shape[2]
    half = rows // 2
    return pl.pallas_call(
        partial_kernel,
        out_shape=jax.ShapeDtypeStruct((TP, requests + 2, half, HD), jnp.bfloat16),
        grid_spec=pltpu.PrefetchScalarGridSpec(
            num_scalar_prefetch=2,
            grid=(requests,),
            in_specs=[
                pl.BlockSpec((1, KVH, rows, HD), lambda r, *_: (r, 0, 0, 0)),
                pl.BlockSpec((1, KVH, rows, HD), lambda r, *_: (0, 0, 0, 0)),
                pl.BlockSpec(memory_space=pl.ANY),
                pl.BlockSpec((2, 1, fresh, KVH * HD), lambda r, *_: (0, r, 0, 0)),
                pl.BlockSpec((2, tokens, KVH * HD), lambda r, *_: (0, 0, 0)),
            ],
            out_specs=pl.BlockSpec((TP, requests + 2, half, HD), lambda r, *_: (0, 0, 0, 0)),
            scratch_shapes=[
                pltpu.VMEM((KVH * HD, KVH * rows), jnp.bfloat16),
                pltpu.VMEM((8, KVH * rows), jnp.float32),
                pltpu.VMEM((requests, 2, positions, KVH * HD), jnp.bfloat16),
                pltpu.SemaphoreType.DMA((requests, 2, 2)),
            ],
        ),
        compiler_params=params(),
        cost_estimate=pl.CostEstimate(
            flops=40 * rows * KVH * positions * HD * requests,
            bytes_accessed=4 * requests * positions * KVH * HD,
            transcendentals=rows * KVH * positions * requests,
        ),
        name="partials",
    )(info, lengths, q, arrival, cache_kv, tail, pre_kv)


def merge_kernel(x_ref, dec_ref, arr_ref):
    lse = x_ref[:, 5].astype(jnp.float32)
    lane = lax.broadcasted_iota(jnp.int32, lse.shape, 2)
    for slot in range(5):
        pick = jnp.logical_and(lane % 8 == slot, lane < 24)
        mine = jnp.sum(jnp.where(pick, lse, 0.0), axis=-1, keepdims=True)
        top = jnp.max(mine, axis=0, keepdims=True)
        w = jnp.exp2(mine - top)
        total = jnp.sum(w, axis=0)
        mixed = jnp.sum(w * x_ref[:, slot].astype(jnp.float32), axis=0) / total
        if slot < 4:
            dec_ref[slot] = mixed.astype(jnp.bfloat16)
        else:
            arr_ref[...] = mixed.astype(jnp.bfloat16)


def merge(x):
    half = x.shape[2]
    return pl.pallas_call(
        merge_kernel,
        out_shape=(
            jax.ShapeDtypeStruct((4, half, HD), jnp.bfloat16),
            jax.ShapeDtypeStruct((half, HD), jnp.bfloat16),
        ),
        name="merge",
    )(x)


def select_kernel(table, x_ref, arr_ref, out_ref):
    tokens = x_ref.shape[1]
    pool = table[2 * POOL * MOST]
    extra = arr_ref.shape[0]
    for d in range(POOL):
        for m in range(MOST):
            prompt = table[d * MOST + m]
            held = table[POOL * MOST + d * MOST + m] == 1
            x = x_ref[pl.ds(prompt, 1)]
            out_ref[d, m, :tokens] = jnp.where(held, x, jnp.zeros_like(x))[0]
            row = jnp.where(
                jnp.logical_and(held, prompt == pool), arr_ref[...], jnp.zeros_like(arr_ref)
            )
            out_ref[d, m, tokens:, :HD] = row
            out_ref[d, m, tokens:, HD:] = jnp.zeros((extra, x.shape[2] - HD), jnp.bfloat16)


def select(table, pieces, arrived):
    _, tokens, width = pieces.shape
    extra = arrived.shape[0]
    return pl.pallas_call(
        select_kernel,
        out_shape=jax.ShapeDtypeStruct((POOL, MOST, tokens + extra, width), jnp.bfloat16),
        in_specs=[
            pl.BlockSpec(memory_space=pltpu.SMEM),
            pl.BlockSpec(memory_space=pltpu.VMEM),
            pl.BlockSpec(memory_space=pltpu.VMEM),
        ],
        out_specs=pl.BlockSpec(memory_space=pltpu.VMEM),
        compiler_params=params(),
        name="select",
    )(table, pieces, arrived)


def settle_kernel(table, x_ref, kv_ref, arr_ref):
    tokens = kv_ref.shape[2]
    width = x_ref.shape[3]
    pool = table[2 * POOL * MOST]
    for m in range(MOST):
        for i in range(POOL):
            at = i % 4 * width
            kv_ref[i // 4, m, :, at : at + width] = x_ref[i, m, :tokens]
        prompt = table[pool * MOST + m]
        arr_ref[m] = x_ref[pl.ds(prompt, 1), m, tokens:, :HD][0]


def settle(table, x):
    _, _, rows, width = x.shape
    tokens = rows - 16
    return pl.pallas_call(
        settle_kernel,
        out_shape=(
            jax.ShapeDtypeStruct((2, MOST, tokens, KVH * HD), jnp.bfloat16),
            jax.ShapeDtypeStruct((MOST, rows - tokens, HD), jnp.bfloat16),
        ),
        in_specs=[
            pl.BlockSpec(memory_space=pltpu.SMEM),
            pl.BlockSpec(memory_space=pltpu.VMEM),
        ],
        out_specs=(
            pl.BlockSpec(memory_space=pltpu.VMEM),
            pl.BlockSpec(memory_space=pltpu.VMEM),
        ),
        compiler_params=params(),
        name="settle",
    )(table, x)


def body(pre_q, pre_kv, arrival_q, owner, cache_kv, lengths, dec_q, new_kv):
    tokens = pre_q.shape[0]
    me = lax.axis_index("tp").astype(jnp.int32)
    pool = lax.axis_index("pool").astype(jnp.int32)
    x, y = me // 4, me // 2 % 2
    flags = [x >= 1, x >= 2, x == 3, y == 1]
    info = jnp.stack([me, me % 2] + [f.astype(jnp.int32) for f in flags])
    back1, back2, wrapped, upper = 2, 3, 4, 5

    def permute(a, pairs):
        return lax.ppermute(a, "tp", pairs)

    swap = [(t, t ^ 1) for t in range(TP)]
    across = [(t, t ^ 2) for t in range(TP)]
    forward = [(t, t + 4) for t in range(12)]
    around = [(t, t + 12) for t in range(4)]

    at = np.arange(REP * tokens) % tokens
    sides = jnp.stack([me % 2, 1 - me % 2]) * tokens
    pos = (sides[:, None] + at[None]).astype(jnp.int32).reshape(2, -1, COLS)

    prompts = jnp.arange(owner.shape[0])
    earlier = jnp.logical_and(
        owner[:, None] == owner[None, :], prompts[None, :] < prompts[:, None]
    )
    rank = jnp.sum(earlier.astype(jnp.int32), axis=1)
    hit = jnp.logical_and(
        owner[None, None, :] == jnp.arange(POOL)[:, None, None],
        rank[None, None, :] == jnp.arange(MOST)[None, :, None],
    )
    held = jnp.any(hit, axis=-1).astype(jnp.int32)
    prompt_of = jnp.sum(hit.astype(jnp.int32) * prompts, axis=-1).astype(jnp.int32)
    table = jnp.concatenate([prompt_of.reshape(-1), held.reshape(-1), pool[None]])

    requests = lengths.shape[0]
    dec_rows = dec_q.reshape(STEPS, requests, KVH, 2, REP // 2, HD)
    dec_rows = jnp.transpose(dec_rows, (1, 2, 3, 0, 4, 5)).reshape(requests, KVH, STEPS * REP, HD)
    arrival = lax.dynamic_index_in_dim(arrival_q, pool, 0, False)
    arrival = arrival.reshape(KVH, 2, 1, REP // 2, HD)
    arrival = jnp.pad(arrival, ((0, 0), (0, 0), (0, STEPS - 1), (0, 0), (0, 0)))
    arrival = arrival.reshape(1, KVH, STEPS * REP, HD)
    tail = jnp.pad(jnp.transpose(new_kv, (0, 2, 1, 3)), ((0, 0), (0, 0), (0, 12), (0, 0)))

    kv_own, kv_send, pieces = prep_kv(info, pre_kv)
    kv_swapped = permute(kv_send, swap)
    pieces = lax.all_to_all(pieces, "pool", 0, 0)
    q_send = other_half(info, pre_q)
    own = jnp.stack([kv_own, kv_swapped])
    own, q_send, pieces, info_decode = lax.optimization_barrier((own, q_send, pieces, info))

    a1 = permute(own, forward)
    b0 = permute(own, across)
    w1 = permute(own, around)
    q_sib = permute(q_send, swap)
    part = partials(info_decode, lengths, dec_rows, arrival, cache_kv, tail, pre_kv)
    part = lax.all_to_all(part, "tp", 0, 0)
    part, a1, b0, w1, own, q_sib, info = lax.optimization_barrier(
        (part, a1, b0, w1, own, q_sib, info)
    )

    def take(order, parts, kinds, carry, last):
        return prefill(order, pos, pre_q, q_sib, parts, kinds, carry, last)

    a2 = permute(a1, forward[4:])
    b1 = permute(a1, across[4:])
    w2 = permute(b0, around)
    carry = take(info, [own, a1, b0, w1], [-1, back1, upper, wrapped], None, False)
    decoded, arrived = merge(part)
    arrived, pieces, carry, a2, b1, w2, info = lax.optimization_barrier(
        (arrived, pieces, carry, a2, b1, w2, info)
    )

    b2 = permute(b1, forward[4:])
    landed = lax.all_to_all(select(table, pieces, arrived), "pool", 0, 0)
    carry = take(info, [a2, b1, w2], [back2, back1, wrapped], carry, False)
    carry, b2, landed, info = lax.optimization_barrier((carry, b2, landed, info))

    out, out_send = take(info, [b2], [back2], carry, True)
    received, arrival_rows = settle(table, landed)
    prefill_out = place(info, out, permute(out_send, swap))
    arrival_out = arrival_rows[:, : REP // 2].reshape(MOST, REP // 2 * HD)
    decode_out = jnp.transpose(
        decoded.reshape(requests, STEPS, REP // 2, HD), (1, 0, 2, 3)
    ).reshape(STEPS, requests, REP // 2 * HD)
    return (prefill_out, received, decode_out, arrival_out)


def solution(mesh):
    in_specs = (
        P(("pool", "tp"), None),
        P(None, ("pool", "tp"), None),
        P(),
        P(),
        P(None, "pool", "tp", None),
        P("pool"),
        P(None, "pool", None),
        P(None, None, "pool", None),
    )
    out_specs = (
        P(("pool", "tp"), None),
        P(None, "pool", "tp", None),
        P(None, "pool", "tp"),
        P("pool", "tp"),
    )
    return jax.shard_map(body, mesh=mesh, in_specs=in_specs, out_specs=out_specs, check_vma=False)
```

```python
import functools
import math

import jax
import jax.numpy as jnp
import numpy as np
from jax import lax
from jax.experimental import pallas as pl
from jax.experimental.pallas import tpu as pltpu
from jax.sharding import PartitionSpec as P

H = 64
KVH = 8
REP = H // KVH
HD = 128
STEPS = 4
MOST = 2
POOL = 8
TP = 16
HALF = KVH // 2
NEGATIVE = -1e30
FLOOR = -1e29
SCALE2 = math.log2(math.e) / math.sqrt(HD)
LOG2E = math.log2(math.e)
TILE = 512
UNIT = 64
COLS = 256
VMEM_BYTES = 48 * 1024 * 1024


def params(limit=VMEM_BYTES):
    return pltpu.CompilerParams(vmem_limit_bytes=limit)


def dot_nt(a, b):
    return lax.dot_general(a, b, (((1,), (1,)), ((), ())), preferred_element_type=jnp.float32)


def dot_nn(a, b):
    return lax.dot_general(a, b, (((1,), (0,)), ((), ())), preferred_element_type=jnp.float32)


def prep_kv_kernel(info, kv_ref, own_ref, sib_ref, piece_ref):
    core = info[1]
    for g in range(HALF):
        for half, ref in ((core, own_ref), (1 - core, sib_ref)):
            at = pl.multiple_of((half * HALF + g) * HD, HD)
            ref[g] = kv_ref[:, :, pl.ds(at, HD)]
    width = piece_ref.shape[2]
    for i in range(POOL):
        at = i % 4 * width
        piece_ref[i] = kv_ref[i // 4, :, at : at + width]


def prep_kv(info, pre_kv):
    _, tokens, width = pre_kv.shape
    half = jax.ShapeDtypeStruct((HALF, 2, tokens, HD), jnp.bfloat16)
    return pl.pallas_call(
        prep_kv_kernel,
        out_shape=(half, half, jax.ShapeDtypeStruct((POOL, tokens, width // 4), jnp.bfloat16)),
        grid_spec=pltpu.PrefetchScalarGridSpec(
            num_scalar_prefetch=1,
            grid=(1,),
            in_specs=[pl.BlockSpec((2, tokens, width), lambda i, s: (0, 0, 0))],
            out_specs=(
                pl.BlockSpec((HALF, 2, tokens, HD), lambda i, s: (0, 0, 0, 0)),
                pl.BlockSpec((HALF, 2, tokens, HD), lambda i, s: (0, 0, 0, 0)),
                pl.BlockSpec((POOL, tokens, width // 4), lambda i, s: (0, 0, 0)),
            ),
        ),
        compiler_params=params(),
        name="prep_kv",
    )(info, pre_kv)


def copy_kernel(info, x_ref, out_ref):
    out_ref[...] = x_ref[...]


def other_half(info, pre_q):
    tokens = pre_q.shape[0]
    return pl.pallas_call(
        copy_kernel,
        out_shape=jax.ShapeDtypeStruct((tokens, HALF * REP * HD), jnp.bfloat16),
        grid_spec=pltpu.PrefetchScalarGridSpec(
            num_scalar_prefetch=1,
            grid=(2,),
            in_specs=[
                pl.BlockSpec((tokens, 2 * REP * HD), lambda g, s: (0, (1 - s[1]) * 2 + g))
            ],
            out_specs=pl.BlockSpec((tokens, 2 * REP * HD), lambda g, s: (0, g)),
        ),
        compiler_params=params(),
        name="other_half",
    )(info, pre_q)


def place_kernel(info, kept_ref, x_ref, out_ref):
    del kept_ref
    out_ref[...] = x_ref[...]


def place(info, out, x):
    tokens, width = x.shape
    return pl.pallas_call(
        place_kernel,
        out_shape=jax.ShapeDtypeStruct(out.shape, out.dtype),
        grid_spec=pltpu.PrefetchScalarGridSpec(
            num_scalar_prefetch=1,
            grid=(5,),
            in_specs=[
                pl.BlockSpec(memory_space=pl.ANY),
                pl.BlockSpec((tokens // 5, width), lambda i, s: (i, 0)),
            ],
            out_specs=pl.BlockSpec((tokens // 5, width), lambda i, s: (i, 1 - s[1])),
        ),
        input_output_aliases={1: 0},
        compiler_params=params(),
        name="place",
    )(info, out, x)


def prefill_kernel(info, pos_ref, qa_ref, qb_ref, *refs, kinds, first, last):
    count = len(kinds)
    parts, refs = refs[:count], refs[count:]
    if not first:
        carry, refs = ((refs[0], refs[1]), (refs[2], refs[3])), refs[4:]
    if last:
        outs, refs = refs[:2], refs[2:]
    else:
        outs, refs = ((refs[0], refs[1]), (refs[2], refs[3])), refs[4:]
    k_all, v_all, v_across, q_all, s_all, top_all = refs[:6]
    g = pl.program_id(0)
    heads = pl.num_programs(0) - 1
    core = info[1]
    tokens = parts[0].shape[3]
    shard = 2 * tokens
    keys = count * shard
    blocks = q_all.shape[1] // COLS
    tiles = [(lo, min(lo + TILE, keys)) for lo in range(0, keys, TILE)]
    valid = [None if kind < 0 else info[kind] == 1 for kind in kinds]

    def load():
        for h in range(REP):
            at = h * tokens
            q_all[0, at : at + tokens, :] = qa_ref[:, h * HD : (h + 1) * HD]
            q_all[1, at : at + tokens, :] = qb_ref[:, h * HD : (h + 1) * HD]
        for i, part in enumerate(parts):
            for k in range(2):
                at = i * shard + k * tokens
                k_all[at : at + tokens, :] = part[k, 0, 0]
                v_all[at : at + tokens, :] = part[k, 0, 1]
        if v_all.shape[0] > keys:
            v_all[keys:, :] = jnp.zeros((v_all.shape[0] - keys, HD), jnp.bfloat16)
        for at in range(0, v_all.shape[0], 128):
            v_across[g % 2, :, at : at + 128] = v_all[at : at + 128, :].T

    def scores(side, n):
        q = q_all[side, n * COLS : (n + 1) * COLS, :]
        top = None
        for lo, hi in tiles:
            s = dot_nt(k_all[lo:hi, :], q)
            for at in range(lo, hi, UNIT):
                piece = s[at - lo : at - lo + UNIT, :]
                which = at // shard
                if valid[which] is None:
                    key = lax.broadcasted_iota(jnp.int32, piece.shape, 0) + (at - which * shard)
                    key = jnp.where(key < tokens, key + core * tokens, key - core * tokens)
                    seen = key <= pos_ref[side, n : n + 1, :]
                    piece = jnp.where(seen, piece, NEGATIVE)
                s_all[side, n, at : at + UNIT, :] = piece
                part = jnp.max(piece.reshape(UNIT // 8, 8, COLS), axis=0)
                if valid[which] is not None:
                    part = jnp.where(valid[which], part, NEGATIVE)
                top = part if top is None else jnp.maximum(top, part)
            yield
        top_all[side, n] = top

    def finish(side, n, slot):
        peak = jnp.max(top_all[side, n], axis=0, keepdims=True)
        if not first:
            acc_in, stat_in = carry[side]
            before = stat_in[0, n, 0:1, :]
            peak = jnp.maximum(before, peak)
            shrink = jnp.exp2((before - peak) * SCALE2)
        total = None
        acc = None
        for lo, hi in tiles:
            rounded = []
            for at in range(lo, hi, UNIT):
                which = at // shard
                base = peak if valid[which] is None else jnp.where(valid[which], peak, -NEGATIVE)
                w = jnp.exp2((s_all[side, n, at : at + UNIT, :] - base) * SCALE2)
                part = jnp.sum(w.reshape(UNIT // 8, 8, COLS), axis=0)
                total = part if total is None else total + part
                rounded.append(w.astype(jnp.bfloat16))
            w = jnp.concatenate(rounded, axis=0)
            part = dot_nn(v_across[slot, :, lo:hi], w)
            acc = part if acc is None else acc + part
            yield
        total = jnp.sum(total, axis=0, keepdims=True)
        if not first:
            acc = acc + acc_in[0, n].astype(jnp.float32) * shrink
            total = total + stat_in[0, n, 1:2, :] * shrink
        if last:
            stage = refs[6]
            stage[side, n * COLS : (n + 1) * COLS, :] = (acc * (1.0 / total)).T.astype(jnp.bfloat16)
        else:
            acc_out, stat_out = outs[side]
            acc_out[0, n] = acc.astype(jnp.bfloat16)
            line = lax.broadcasted_iota(jnp.int32, (8, COLS), 0)
            stat_out[0, n] = jnp.where(line == 0, peak, total)

    def drain(steps):
        live = list(steps)
        while live:
            for step in list(live):
                if next(step, live) is live:
                    live.remove(step)

    def both(scored, finished, slot):
        if scored == 0:
            load()
        for n in range(blocks):
            steps = [] if scored is None else [scores(scored, n)]
            if finished is not None:
                steps.append(finish(finished, n, slot))
            drain(steps)
        if last and finished is not None:
            stage = refs[6]
            for h in range(REP):
                at = h * tokens
                outs[finished][:, h * HD : (h + 1) * HD] = stage[finished, at : at + tokens, :]

    before = (g + 1) % 2
    pl.when(g == 0)(lambda: both(0, None, None))
    pl.when(jnp.logical_and(g > 0, g < heads))(lambda: both(0, 1, before))
    pl.when(g == heads)(lambda: both(None, 1, before))
    pl.when(g < heads)(lambda: both(1, 0, g % 2))


def prefill(info, pos, pre_q, q_sib, parts, kinds, carry, last):
    tokens = pre_q.shape[0]
    rows = REP * tokens
    blocks = rows // COLS
    first = carry is None
    keys = len(parts) * 2 * tokens
    room = -(-keys // 128) * 128

    def now(g):
        return jnp.minimum(g, HALF - 1)

    def late(g):
        return jnp.maximum(g - 1, 0)

    in_specs = [
        pl.BlockSpec(pos.shape, lambda g, s: (0, 0, 0)),
        pl.BlockSpec((tokens, REP * HD), lambda g, s: (0, s[1] * HALF + now(g))),
        pl.BlockSpec((tokens, REP * HD), lambda g, s: (0, now(g))),
    ]
    in_specs += [
        pl.BlockSpec((2, 1, 2, tokens, HD), lambda g, s: (0, now(g), 0, 0, 0)) for _ in parts
    ]
    args = [pos, pre_q, q_sib, *parts]
    carry_specs = [
        pl.BlockSpec((1, blocks, HD, COLS), lambda g, s: (now(g), 0, 0, 0)),
        pl.BlockSpec((1, blocks, 8, COLS), lambda g, s: (now(g), 0, 0, 0)),
        pl.BlockSpec((1, blocks, HD, COLS), lambda g, s: (late(g), 0, 0, 0)),
        pl.BlockSpec((1, blocks, 8, COLS), lambda g, s: (late(g), 0, 0, 0)),
    ]
    if not first:
        in_specs += carry_specs
        args += list(carry)
    scratch = [
        pltpu.VMEM((keys, HD), jnp.bfloat16),
        pltpu.VMEM((room, HD), jnp.bfloat16),
        pltpu.VMEM((2, HD, room), jnp.bfloat16),
        pltpu.VMEM((2, rows, HD), jnp.bfloat16),
        pltpu.VMEM((2, blocks, keys, COLS), jnp.float32),
        pltpu.VMEM((2, blocks, 8, COLS), jnp.float32),
    ]
    if last:
        out_shape = [
            jax.ShapeDtypeStruct(pre_q.shape, jnp.bfloat16),
            jax.ShapeDtypeStruct(q_sib.shape, jnp.bfloat16),
        ]
        out_specs = [
            pl.BlockSpec((tokens, REP * HD), lambda g, s: (0, s[1] * HALF + now(g))),
            pl.BlockSpec((tokens, REP * HD), lambda g, s: (0, late(g))),
        ]
        scratch.append(pltpu.VMEM((2, rows, HD), jnp.bfloat16))
    else:
        out_shape = [
            jax.ShapeDtypeStruct((HALF, blocks, HD, COLS), jnp.bfloat16),
            jax.ShapeDtypeStruct((HALF, blocks, 8, COLS), jnp.float32),
        ] * 2
        out_specs = carry_specs
    return pl.pallas_call(
        functools.partial(prefill_kernel, kinds=kinds, first=first, last=last),
        out_shape=out_shape,
        grid_spec=pltpu.PrefetchScalarGridSpec(
            num_scalar_prefetch=1,
            grid=(HALF + 1,),
            in_specs=in_specs,
            out_specs=out_specs,
            scratch_shapes=scratch,
        ),
        compiler_params=params(60 * 1024 * 1024),
        cost_estimate=pl.CostEstimate(
            flops=16 * HALF * rows * keys * HD,
            bytes_accessed=24 * HALF * rows * HD,
            transcendentals=2 * HALF * rows * keys,
        ),
        name="prefill",
    )(info, *args)


def partial_kernel(
    info, lens, q_ref, aq_ref, cache, tail_ref, pre_ref, out_ref, q_wide, lse_ref, held, sems
):
    me = info[0]
    r = pl.program_id(0)
    requests, _, positions, _ = held.shape
    fresh = tail_ref.shape[2]
    rows = q_ref.shape[2]
    wide = KVH * rows
    half = rows // 2

    chunk = positions // 2

    def copy(i, j, k):
        some = pl.ds(k * chunk, chunk)
        return pltpu.make_async_copy(
            cache.at[j, i, some], held.at[i, j, some], sems.at[i, j, k]
        )

    @pl.when(r == 0)
    def _():
        for i in range(requests):
            for j in range(2):
                for k in range(2):
                    copy(i, j, k).start()
        q_wide[...] = jnp.zeros_like(q_wide)
        lse_ref[...] = jnp.zeros_like(lse_ref)

    def spread(ref):
        lane = lax.broadcasted_iota(jnp.int32, (HD, 128), 1) // rows
        per = 128 // rows
        for i in range(KVH // per):
            turned = ref[0, i * per : (i + 1) * per].reshape(128, HD).T
            for j in range(per):
                g = i * per + j
                q_wide[g * HD : (g + 1) * HD, i * 128 : (i + 1) * 128] = jnp.where(
                    lane == j, turned, jnp.zeros_like(turned)
                )

    def fold(w):
        return w.reshape(w.shape[0] // 8, 8, wide)

    def weigh(s, t, slot):
        peak = jnp.max(jnp.max(fold(s), axis=0), axis=0, keepdims=True)
        if t is not None:
            peak = jnp.maximum(peak, jnp.max(t, axis=0, keepdims=True))
            peak = jnp.maximum(peak, FLOOR)
        s = jnp.exp2((s - peak) * SCALE2)
        total = jnp.sum(jnp.sum(fold(s), axis=0), axis=0, keepdims=True)
        if t is not None:
            t = jnp.exp2((t - peak) * SCALE2)
            total = total + jnp.sum(t, axis=0, keepdims=True)
        live = total > 0.0
        safe = jnp.where(live, total, 1.0)
        lse_ref[pl.ds(slot, 1), :] = jnp.where(
            live, peak * SCALE2 + jnp.log(safe) * LOG2E, NEGATIVE
        )
        share = jnp.where(live, 1.0 / safe, 0.0)
        s = (s * share).astype(jnp.bfloat16)
        return s, None if t is None else t * share

    def store(g, slot, mean):
        mean = mean.astype(jnp.bfloat16)
        for k in range(2):
            out_ref[2 * g + k, pl.ds(slot, 1)] = mean[k * half : (k + 1) * half][None]

    @pl.when(r == 0)
    def _():
        spread(aq_ref)
        tokens = pre_ref.shape[1]
        w, _ = weigh(dot_nn(pre_ref[0], q_wide[...]), None, 4)
        w = jnp.concatenate([w, jnp.zeros((256 - tokens, wide), jnp.bfloat16)], axis=0).T
        for g in range(KVH):
            values = pre_ref[1, :, g * HD : (g + 1) * HD]
            store(g, 4, dot_nn(w[g * rows : (g + 1) * rows, :tokens], values))

    spread(q_ref)
    q = q_wide[...]
    for j in range(2):
        for k in range(2):
            copy(r, j, k).wait()
    shown = lax.broadcasted_iota(jnp.int32, (positions, wide), 0) < lens[r] - me * positions
    s = jnp.where(shown, dot_nn(held[r, 0], q), NEGATIVE)
    step = lax.broadcasted_iota(jnp.int32, (fresh, wide), 1) % half // (half // STEPS)
    at = lax.broadcasted_iota(jnp.int32, (fresh, wide), 0)
    tail_shown = jnp.logical_and(at <= step, me == 0)
    t = jnp.where(tail_shown, dot_nn(tail_ref[0, 0], q), NEGATIVE)
    w, u = weigh(s, t, r)
    w = w.T
    u = jnp.concatenate([u, jnp.zeros((128 - fresh, wide), jnp.float32)], axis=0).T
    u = u.astype(jnp.bfloat16)
    for g in range(KVH):
        cols = slice(g * HD, (g + 1) * HD)
        mine = slice(g * rows, (g + 1) * rows)
        mean = dot_nn(w[mine, :], held[r, 1, :, cols])
        store(g, r, mean + dot_nn(u[mine, :fresh], tail_ref[1, 0, :, cols]))

    @pl.when(r == pl.num_programs(0) - 1)
    def _():
        x = lse_ref[...]
        high = x.astype(jnp.bfloat16).astype(jnp.float32)
        mid = (x - high).astype(jnp.bfloat16).astype(jnp.float32)
        low = x - high - mid
        rest = jnp.zeros((128 - 3 * x.shape[0], wide), jnp.float32)
        lines = jnp.concatenate([high, mid, low, rest], axis=0).T.astype(jnp.bfloat16)
        for d in range(TP):
            out_ref[d, 5] = lines[d * half : (d + 1) * half, :]


def partials(info, lengths, q, arrival, cache_kv, tail, pre_kv):
    requests = lengths.shape[0]
    positions = cache_kv.shape[2]
    tokens = pre_kv.shape[1]
    fresh = tail.shape[2]
    rows = q.shape[2]
    half = rows // 2
    return pl.pallas_call(
        partial_kernel,
        out_shape=jax.ShapeDtypeStruct((TP, requests + 2, half, HD), jnp.bfloat16),
        grid_spec=pltpu.PrefetchScalarGridSpec(
            num_scalar_prefetch=2,
            grid=(requests,),
            in_specs=[
                pl.BlockSpec((1, KVH, rows, HD), lambda r, *_: (r, 0, 0, 0)),
                pl.BlockSpec((1, KVH, rows, HD), lambda r, *_: (0, 0, 0, 0)),
                pl.BlockSpec(memory_space=pl.ANY),
                pl.BlockSpec((2, 1, fresh, KVH * HD), lambda r, *_: (0, r, 0, 0)),
                pl.BlockSpec((2, tokens, KVH * HD), lambda r, *_: (0, 0, 0)),
            ],
            out_specs=pl.BlockSpec((TP, requests + 2, half, HD), lambda r, *_: (0, 0, 0, 0)),
            scratch_shapes=[
                pltpu.VMEM((KVH * HD, KVH * rows), jnp.bfloat16),
                pltpu.VMEM((8, KVH * rows), jnp.float32),
                pltpu.VMEM((requests, 2, positions, KVH * HD), jnp.bfloat16),
                pltpu.SemaphoreType.DMA((requests, 2, 2)),
            ],
        ),
        compiler_params=params(),
        cost_estimate=pl.CostEstimate(
            flops=40 * rows * KVH * positions * HD * requests,
            bytes_accessed=4 * requests * positions * KVH * HD,
            transcendentals=rows * KVH * positions * requests,
        ),
        name="partials",
    )(info, lengths, q, arrival, cache_kv, tail, pre_kv)


def merge_kernel(x_ref, dec_ref, arr_ref):
    lse = x_ref[:, 5].astype(jnp.float32)
    lane = lax.broadcasted_iota(jnp.int32, lse.shape, 2)
    for slot in range(5):
        pick = jnp.logical_and(lane % 8 == slot, lane < 24)
        mine = jnp.sum(jnp.where(pick, lse, 0.0), axis=-1, keepdims=True)
        top = jnp.max(mine, axis=0, keepdims=True)
        w = jnp.exp2(mine - top)
        total = jnp.sum(w, axis=0)
        mixed = jnp.sum(w * x_ref[:, slot].astype(jnp.float32), axis=0) / total
        if slot < 4:
            dec_ref[slot] = mixed.astype(jnp.bfloat16)
        else:
            arr_ref[...] = mixed.astype(jnp.bfloat16)


def merge(x):
    half = x.shape[2]
    return pl.pallas_call(
        merge_kernel,
        out_shape=(
            jax.ShapeDtypeStruct((4, half, HD), jnp.bfloat16),
            jax.ShapeDtypeStruct((half, HD), jnp.bfloat16),
        ),
        name="merge",
    )(x)


def select_kernel(table, x_ref, arr_ref, out_ref):
    tokens = x_ref.shape[1]
    pool = table[2 * POOL * MOST]
    extra = arr_ref.shape[0]
    for d in range(POOL):
        for m in range(MOST):
            prompt = table[d * MOST + m]
            held = table[POOL * MOST + d * MOST + m] == 1
            x = x_ref[pl.ds(prompt, 1)]
            out_ref[d, m, :tokens] = jnp.where(held, x, jnp.zeros_like(x))[0]
            row = jnp.where(
                jnp.logical_and(held, prompt == pool), arr_ref[...], jnp.zeros_like(arr_ref)
            )
            out_ref[d, m, tokens:, :HD] = row
            out_ref[d, m, tokens:, HD:] = jnp.zeros((extra, x.shape[2] - HD), jnp.bfloat16)


def select(table, pieces, arrived):
    _, tokens, width = pieces.shape
    extra = arrived.shape[0]
    return pl.pallas_call(
        select_kernel,
        out_shape=jax.ShapeDtypeStruct((POOL, MOST, tokens + extra, width), jnp.bfloat16),
        in_specs=[
            pl.BlockSpec(memory_space=pltpu.SMEM),
            pl.BlockSpec(memory_space=pltpu.VMEM),
            pl.BlockSpec(memory_space=pltpu.VMEM),
        ],
        out_specs=pl.BlockSpec(memory_space=pltpu.VMEM),
        compiler_params=params(),
        name="select",
    )(table, pieces, arrived)


def settle_kernel(table, x_ref, kv_ref, arr_ref):
    tokens = kv_ref.shape[2]
    width = x_ref.shape[3]
    pool = table[2 * POOL * MOST]
    for m in range(MOST):
        for i in range(POOL):
            at = i % 4 * width
            kv_ref[i // 4, m, :, at : at + width] = x_ref[i, m, :tokens]
        prompt = table[pool * MOST + m]
        arr_ref[m] = x_ref[pl.ds(prompt, 1), m, tokens:, :HD][0]


def settle(table, x):
    _, _, rows, width = x.shape
    tokens = rows - 16
    return pl.pallas_call(
        settle_kernel,
        out_shape=(
            jax.ShapeDtypeStruct((2, MOST, tokens, KVH * HD), jnp.bfloat16),
            jax.ShapeDtypeStruct((MOST, rows - tokens, HD), jnp.bfloat16),
        ),
        in_specs=[
            pl.BlockSpec(memory_space=pltpu.SMEM),
            pl.BlockSpec(memory_space=pltpu.VMEM),
        ],
        out_specs=(
            pl.BlockSpec(memory_space=pltpu.VMEM),
            pl.BlockSpec(memory_space=pltpu.VMEM),
        ),
        compiler_params=params(),
        name="settle",
    )(table, x)


def body(pre_q, pre_kv, arrival_q, owner, cache_kv, lengths, dec_q, new_kv):
    tokens = pre_q.shape[0]
    me = lax.axis_index("tp").astype(jnp.int32)
    pool = lax.axis_index("pool").astype(jnp.int32)
    x, y = me // 4, me // 2 % 2
    flags = [x >= 1, x >= 2, x == 3, y == 1]
    info = jnp.stack([me, me % 2] + [f.astype(jnp.int32) for f in flags])
    back1, back2, wrapped, upper = 2, 3, 4, 5

    def permute(a, pairs):
        return lax.ppermute(a, "tp", pairs)

    swap = [(t, t ^ 1) for t in range(TP)]
    across = [(t, t ^ 2) for t in range(TP)]
    forward = [(t, t + 4) for t in range(12)]
    around = [(t, t + 12) for t in range(4)]

    at = np.arange(REP * tokens) % tokens
    sides = jnp.stack([me % 2, 1 - me % 2]) * tokens
    pos = (sides[:, None] + at[None]).astype(jnp.int32).reshape(2, -1, COLS)

    prompts = jnp.arange(owner.shape[0])
    earlier = jnp.logical_and(
        owner[:, None] == owner[None, :], prompts[None, :] < prompts[:, None]
    )
    rank = jnp.sum(earlier.astype(jnp.int32), axis=1)
    hit = jnp.logical_and(
        owner[None, None, :] == jnp.arange(POOL)[:, None, None],
        rank[None, None, :] == jnp.arange(MOST)[None, :, None],
    )
    held = jnp.any(hit, axis=-1).astype(jnp.int32)
    prompt_of = jnp.sum(hit.astype(jnp.int32) * prompts, axis=-1).astype(jnp.int32)
    table = jnp.concatenate([prompt_of.reshape(-1), held.reshape(-1), pool[None]])

    requests = lengths.shape[0]
    dec_rows = dec_q.reshape(STEPS, requests, KVH, 2, REP // 2, HD)
    dec_rows = jnp.transpose(dec_rows, (1, 2, 3, 0, 4, 5)).reshape(requests, KVH, STEPS * REP, HD)
    arrival = lax.dynamic_index_in_dim(arrival_q, pool, 0, False)
    arrival = arrival.reshape(KVH, 2, 1, REP // 2, HD)
    arrival = jnp.pad(arrival, ((0, 0), (0, 0), (0, STEPS - 1), (0, 0), (0, 0)))
    arrival = arrival.reshape(1, KVH, STEPS * REP, HD)
    tail = jnp.pad(jnp.transpose(new_kv, (0, 2, 1, 3)), ((0, 0), (0, 0), (0, 12), (0, 0)))

    kv_own, kv_send, pieces = prep_kv(info, pre_kv)
    kv_swapped = permute(kv_send, swap)
    q_send = other_half(info, pre_q)
    own = jnp.stack([kv_own, kv_swapped])
    own, q_send, info_decode = lax.optimization_barrier((own, q_send, info))

    a1 = permute(own, forward)
    b0 = permute(own, across)
    w1 = permute(own, around)
    q_sib = permute(q_send, swap)
    part = partials(info_decode, lengths, dec_rows, arrival, cache_kv, tail, pre_kv)
    part, a1, b0, w1, own, q_sib, info = lax.optimization_barrier(
        (part, a1, b0, w1, own, q_sib, info)
    )

    def take(order, parts, kinds, carry, last):
        return prefill(order, pos, pre_q, q_sib, parts, kinds, carry, last)

    a2 = permute(a1, forward[4:])
    b1 = permute(a1, across[4:])
    w2 = permute(b0, around)
    part = lax.all_to_all(part, "tp", 0, 0)
    part, pieces, info = lax.optimization_barrier((part, pieces, info))
    pieces = lax.all_to_all(pieces, "pool", 0, 0)
    carry = take(info, [own, a1, b0, w1], [-1, back1, upper, wrapped], None, False)
    part, pieces, carry, a2, b1, w2, info = lax.optimization_barrier(
        (part, pieces, carry, a2, b1, w2, info)
    )
    decoded, arrived = merge(part)

    b2 = permute(b1, forward[4:])
    landed = lax.all_to_all(select(table, pieces, arrived), "pool", 0, 0)
    carry = take(info, [a2, b1, w2], [back2, back1, wrapped], carry, False)
    carry, b2, landed, info = lax.optimization_barrier((carry, b2, landed, info))

    out, out_send = take(info, [b2], [back2], carry, True)
    received, arrival_rows = settle(table, landed)
    prefill_out = place(info, out, permute(out_send, swap))
    arrival_out = arrival_rows[:, : REP // 2].reshape(MOST, REP // 2 * HD)
    decode_out = jnp.transpose(
        decoded.reshape(requests, STEPS, REP // 2, HD), (1, 0, 2, 3)
    ).reshape(STEPS, requests, REP // 2 * HD)
    return (prefill_out, received, decode_out, arrival_out)


def solution(mesh):
    in_specs = (
        P(("pool", "tp"), None),
        P(None, ("pool", "tp"), None),
        P(),
        P(),
        P(None, "pool", "tp", None),
        P("pool"),
        P(None, "pool", None),
        P(None, None, "pool", None),
    )
    out_specs = (
        P(("pool", "tp"), None),
        P(None, "pool", "tp", None),
        P(None, "pool", "tp"),
        P("pool", "tp"),
    )
    return jax.shard_map(body, mesh=mesh, in_specs=in_specs, out_specs=out_specs, check_vma=False)
```

```python
import functools
import math

import jax
import jax.numpy as jnp
import numpy as np
from jax import lax
from jax.experimental import pallas as pl
from jax.experimental.pallas import tpu as pltpu
from jax.sharding import PartitionSpec as P

H = 64
KVH = 8
REP = H // KVH
HD = 128
STEPS = 4
MOST = 2
POOL = 8
TP = 16
HALF = KVH // 2
NEGATIVE = -1e30
FLOOR = -1e29
SCALE2 = math.log2(math.e) / math.sqrt(HD)
LOG2E = math.log2(math.e)
TILE = 512
UNIT = 64
COLS = 256
VMEM_BYTES = 48 * 1024 * 1024


def params(limit=VMEM_BYTES):
    return pltpu.CompilerParams(vmem_limit_bytes=limit)


def dot_nt(a, b):
    return lax.dot_general(a, b, (((1,), (1,)), ((), ())), preferred_element_type=jnp.float32)


def dot_nn(a, b):
    return lax.dot_general(a, b, (((1,), (0,)), ((), ())), preferred_element_type=jnp.float32)


def prep_kv_kernel(info, kv_ref, own_ref, sib_ref, piece_ref):
    core = info[1]
    for g in range(HALF):
        for half, ref in ((core, own_ref), (1 - core, sib_ref)):
            at = pl.multiple_of((half * HALF + g) * HD, HD)
            ref[g] = kv_ref[:, :, pl.ds(at, HD)]
    width = piece_ref.shape[2]
    for i in range(POOL):
        at = i % 4 * width
        piece_ref[i] = kv_ref[i // 4, :, at : at + width]


def prep_kv(info, pre_kv):
    _, tokens, width = pre_kv.shape
    half = jax.ShapeDtypeStruct((HALF, 2, tokens, HD), jnp.bfloat16)
    return pl.pallas_call(
        prep_kv_kernel,
        out_shape=(half, half, jax.ShapeDtypeStruct((POOL, tokens, width // 4), jnp.bfloat16)),
        grid_spec=pltpu.PrefetchScalarGridSpec(
            num_scalar_prefetch=1,
            grid=(1,),
            in_specs=[pl.BlockSpec((2, tokens, width), lambda i, s: (0, 0, 0))],
            out_specs=(
                pl.BlockSpec((HALF, 2, tokens, HD), lambda i, s: (0, 0, 0, 0)),
                pl.BlockSpec((HALF, 2, tokens, HD), lambda i, s: (0, 0, 0, 0)),
                pl.BlockSpec((POOL, tokens, width // 4), lambda i, s: (0, 0, 0)),
            ),
        ),
        compiler_params=params(),
        name="prep_kv",
    )(info, pre_kv)


def copy_kernel(info, x_ref, out_ref):
    out_ref[...] = x_ref[...]


def other_half(info, pre_q):
    tokens = pre_q.shape[0]
    return pl.pallas_call(
        copy_kernel,
        out_shape=jax.ShapeDtypeStruct((tokens, HALF * REP * HD), jnp.bfloat16),
        grid_spec=pltpu.PrefetchScalarGridSpec(
            num_scalar_prefetch=1,
            grid=(2,),
            in_specs=[
                pl.BlockSpec((tokens, 2 * REP * HD), lambda g, s: (0, (1 - s[1]) * 2 + g))
            ],
            out_specs=pl.BlockSpec((tokens, 2 * REP * HD), lambda g, s: (0, g)),
        ),
        compiler_params=params(),
        name="other_half",
    )(info, pre_q)


def place_kernel(info, kept_ref, x_ref, out_ref):
    del kept_ref
    out_ref[...] = x_ref[...]


def place(info, out, x):
    tokens, width = x.shape
    return pl.pallas_call(
        place_kernel,
        out_shape=jax.ShapeDtypeStruct(out.shape, out.dtype),
        grid_spec=pltpu.PrefetchScalarGridSpec(
            num_scalar_prefetch=1,
            grid=(5,),
            in_specs=[
                pl.BlockSpec(memory_space=pl.ANY),
                pl.BlockSpec((tokens // 5, width), lambda i, s: (i, 0)),
            ],
            out_specs=pl.BlockSpec((tokens // 5, width), lambda i, s: (i, 1 - s[1])),
        ),
        input_output_aliases={1: 0},
        compiler_params=params(),
        name="place",
    )(info, out, x)


def prefill_kernel(info, pos_ref, qa_ref, qb_ref, *refs, kinds, first, last):
    count = len(kinds)
    parts, refs = refs[:count], refs[count:]
    if not first:
        carry, refs = ((refs[0], refs[1]), (refs[2], refs[3])), refs[4:]
    if last:
        outs, refs = refs[:2], refs[2:]
    else:
        outs, refs = ((refs[0], refs[1]), (refs[2], refs[3])), refs[4:]
    k_all, v_all, v_across, q_all, s_all, top_all = refs[:6]
    g = pl.program_id(0)
    heads = pl.num_programs(0) - 1
    core = info[1]
    tokens = parts[0].shape[3]
    shard = 2 * tokens
    keys = count * shard
    blocks = q_all.shape[1] // COLS
    tiles = [(lo, min(lo + TILE, keys)) for lo in range(0, keys, TILE)]
    valid = [None if kind < 0 else info[kind] == 1 for kind in kinds]

    def load():
        for h in range(REP):
            at = h * tokens
            q_all[0, at : at + tokens, :] = qa_ref[:, h * HD : (h + 1) * HD]
            q_all[1, at : at + tokens, :] = qb_ref[:, h * HD : (h + 1) * HD]
        for i, part in enumerate(parts):
            for k in range(2):
                at = i * shard + k * tokens
                k_all[at : at + tokens, :] = part[k, 0, 0]
                v_all[at : at + tokens, :] = part[k, 0, 1]
        if v_all.shape[0] > keys:
            v_all[keys:, :] = jnp.zeros((v_all.shape[0] - keys, HD), jnp.bfloat16)
        for at in range(0, v_all.shape[0], 128):
            v_across[g % 2, :, at : at + 128] = v_all[at : at + 128, :].T

    def scores(side, n):
        q = q_all[side, n * COLS : (n + 1) * COLS, :]
        top = None
        for lo, hi in tiles:
            s = dot_nt(k_all[lo:hi, :], q)
            for at in range(lo, hi, UNIT):
                piece = s[at - lo : at - lo + UNIT, :]
                which = at // shard
                if valid[which] is None:
                    key = lax.broadcasted_iota(jnp.int32, piece.shape, 0) + (at - which * shard)
                    key = jnp.where(key < tokens, key + core * tokens, key - core * tokens)
                    seen = key <= pos_ref[side, n : n + 1, :]
                    piece = jnp.where(seen, piece, NEGATIVE)
                s_all[side, n, at : at + UNIT, :] = piece
                part = jnp.max(piece.reshape(UNIT // 8, 8, COLS), axis=0)
                if valid[which] is not None:
                    part = jnp.where(valid[which], part, NEGATIVE)
                top = part if top is None else jnp.maximum(top, part)
            yield
        top_all[side, n] = top

    def finish(side, n, slot):
        peak = jnp.max(top_all[side, n], axis=0, keepdims=True)
        if not first:
            acc_in, stat_in = carry[side]
            before = stat_in[0, n, 0:1, :]
            peak = jnp.maximum(before, peak)
            shrink = jnp.exp2((before - peak) * SCALE2)
        total = None
        acc = None
        for lo, hi in tiles:
            rounded = []
            for at in range(lo, hi, UNIT):
                which = at // shard
                base = peak if valid[which] is None else jnp.where(valid[which], peak, -NEGATIVE)
                w = jnp.exp2((s_all[side, n, at : at + UNIT, :] - base) * SCALE2)
                part = jnp.sum(w.reshape(UNIT // 8, 8, COLS), axis=0)
                total = part if total is None else total + part
                rounded.append(w.astype(jnp.bfloat16))
            w = jnp.concatenate(rounded, axis=0)
            part = dot_nn(v_across[slot, :, lo:hi], w)
            acc = part if acc is None else acc + part
            yield
        total = jnp.sum(total, axis=0, keepdims=True)
        if not first:
            acc = acc + acc_in[0, n].astype(jnp.float32) * shrink
            total = total + stat_in[0, n, 1:2, :] * shrink
        if last:
            stage = refs[6]
            stage[side, n * COLS : (n + 1) * COLS, :] = (acc * (1.0 / total)).T.astype(jnp.bfloat16)
        else:
            acc_out, stat_out = outs[side]
            acc_out[0, n] = acc.astype(jnp.bfloat16)
            line = lax.broadcasted_iota(jnp.int32, (8, COLS), 0)
            stat_out[0, n] = jnp.where(line == 0, peak, total)

    def drain(steps):
        live = list(steps)
        while live:
            for step in list(live):
                if next(step, live) is live:
                    live.remove(step)

    def both(scored, finished, slot):
        if scored == 0:
            load()
        for n in range(blocks):
            steps = [] if scored is None else [scores(scored, n)]
            if finished is not None:
                steps.append(finish(finished, n, slot))
            drain(steps)
        if last and finished is not None:
            stage = refs[6]
            for h in range(REP):
                at = h * tokens
                outs[finished][:, h * HD : (h + 1) * HD] = stage[finished, at : at + tokens, :]

    before = (g + 1) % 2
    pl.when(g == 0)(lambda: both(0, None, None))
    pl.when(jnp.logical_and(g > 0, g < heads))(lambda: both(0, 1, before))
    pl.when(g == heads)(lambda: both(None, 1, before))
    pl.when(g < heads)(lambda: both(1, 0, g % 2))


def prefill(info, pos, pre_q, q_sib, parts, kinds, carry, last):
    tokens = pre_q.shape[0]
    rows = REP * tokens
    blocks = rows // COLS
    first = carry is None
    keys = len(parts) * 2 * tokens
    room = -(-keys // 128) * 128

    def now(g):
        return jnp.minimum(g, HALF - 1)

    def late(g):
        return jnp.maximum(g - 1, 0)

    in_specs = [
        pl.BlockSpec(pos.shape, lambda g, s: (0, 0, 0)),
        pl.BlockSpec((tokens, REP * HD), lambda g, s: (0, s[1] * HALF + now(g))),
        pl.BlockSpec((tokens, REP * HD), lambda g, s: (0, now(g))),
    ]
    in_specs += [
        pl.BlockSpec((2, 1, 2, tokens, HD), lambda g, s: (0, now(g), 0, 0, 0)) for _ in parts
    ]
    args = [pos, pre_q, q_sib, *parts]
    carry_specs = [
        pl.BlockSpec((1, blocks, HD, COLS), lambda g, s: (now(g), 0, 0, 0)),
        pl.BlockSpec((1, blocks, 8, COLS), lambda g, s: (now(g), 0, 0, 0)),
        pl.BlockSpec((1, blocks, HD, COLS), lambda g, s: (late(g), 0, 0, 0)),
        pl.BlockSpec((1, blocks, 8, COLS), lambda g, s: (late(g), 0, 0, 0)),
    ]
    if not first:
        in_specs += carry_specs
        args += list(carry)
    scratch = [
        pltpu.VMEM((keys, HD), jnp.bfloat16),
        pltpu.VMEM((room, HD), jnp.bfloat16),
        pltpu.VMEM((2, HD, room), jnp.bfloat16),
        pltpu.VMEM((2, rows, HD), jnp.bfloat16),
        pltpu.VMEM((2, blocks, keys, COLS), jnp.float32),
        pltpu.VMEM((2, blocks, 8, COLS), jnp.float32),
    ]
    if last:
        out_shape = [
            jax.ShapeDtypeStruct(pre_q.shape, jnp.bfloat16),
            jax.ShapeDtypeStruct(q_sib.shape, jnp.bfloat16),
        ]
        out_specs = [
            pl.BlockSpec((tokens, REP * HD), lambda g, s: (0, s[1] * HALF + now(g))),
            pl.BlockSpec((tokens, REP * HD), lambda g, s: (0, late(g))),
        ]
        scratch.append(pltpu.VMEM((2, rows, HD), jnp.bfloat16))
    else:
        out_shape = [
            jax.ShapeDtypeStruct((HALF, blocks, HD, COLS), jnp.bfloat16),
            jax.ShapeDtypeStruct((HALF, blocks, 8, COLS), jnp.float32),
        ] * 2
        out_specs = carry_specs
    return pl.pallas_call(
        functools.partial(prefill_kernel, kinds=kinds, first=first, last=last),
        out_shape=out_shape,
        grid_spec=pltpu.PrefetchScalarGridSpec(
            num_scalar_prefetch=1,
            grid=(HALF + 1,),
            in_specs=in_specs,
            out_specs=out_specs,
            scratch_shapes=scratch,
        ),
        compiler_params=params(60 * 1024 * 1024),
        cost_estimate=pl.CostEstimate(
            flops=16 * HALF * rows * keys * HD,
            bytes_accessed=24 * HALF * rows * HD,
            transcendentals=2 * HALF * rows * keys,
        ),
        name="prefill",
    )(info, *args)


def partial_kernel(
    info, lens, q_ref, aq_ref, cache, tail_ref, pre_ref, out_ref, q_wide, lse_ref, held, sems
):
    me = info[0]
    r = pl.program_id(0)
    requests, _, positions, _ = held.shape
    fresh = tail_ref.shape[2]
    rows = q_ref.shape[2]
    wide = KVH * rows
    half = rows // 2

    chunk = positions // 2

    def copy(i, j, k):
        some = pl.ds(k * chunk, chunk)
        return pltpu.make_async_copy(
            cache.at[j, i, some], held.at[i, j, some], sems.at[i, j, k]
        )

    @pl.when(r == 0)
    def _():
        for i in range(requests):
            for j in range(2):
                for k in range(2):
                    copy(i, j, k).start()
        q_wide[...] = jnp.zeros_like(q_wide)
        lse_ref[...] = jnp.zeros_like(lse_ref)

    def spread(ref):
        lane = lax.broadcasted_iota(jnp.int32, (HD, 128), 1) // rows
        per = 128 // rows
        for i in range(KVH // per):
            turned = ref[0, i * per : (i + 1) * per].reshape(128, HD).T
            for j in range(per):
                g = i * per + j
                q_wide[g * HD : (g + 1) * HD, i * 128 : (i + 1) * 128] = jnp.where(
                    lane == j, turned, jnp.zeros_like(turned)
                )

    def fold(w):
        return w.reshape(w.shape[0] // 8, 8, wide)

    def weigh(s, t, slot):
        peak = jnp.max(jnp.max(fold(s), axis=0), axis=0, keepdims=True)
        if t is not None:
            peak = jnp.maximum(peak, jnp.max(t, axis=0, keepdims=True))
            peak = jnp.maximum(peak, FLOOR)
        s = jnp.exp2((s - peak) * SCALE2)
        total = jnp.sum(jnp.sum(fold(s), axis=0), axis=0, keepdims=True)
        if t is not None:
            t = jnp.exp2((t - peak) * SCALE2)
            total = total + jnp.sum(t, axis=0, keepdims=True)
        live = total > 0.0
        safe = jnp.where(live, total, 1.0)
        lse_ref[pl.ds(slot, 1), :] = jnp.where(
            live, peak * SCALE2 + jnp.log(safe) * LOG2E, NEGATIVE
        )
        share = jnp.where(live, 1.0 / safe, 0.0)
        s = (s * share).astype(jnp.bfloat16)
        return s, None if t is None else t * share

    def store(g, slot, mean):
        mean = mean.astype(jnp.bfloat16)
        for k in range(2):
            out_ref[2 * g + k, pl.ds(slot, 1)] = mean[k * half : (k + 1) * half][None]

    @pl.when(r == 0)
    def _():
        spread(aq_ref)
        tokens = pre_ref.shape[1]
        w, _ = weigh(dot_nn(pre_ref[0], q_wide[...]), None, 4)
        w = jnp.concatenate([w, jnp.zeros((256 - tokens, wide), jnp.bfloat16)], axis=0).T
        for g in range(KVH):
            values = pre_ref[1, :, g * HD : (g + 1) * HD]
            store(g, 4, dot_nn(w[g * rows : (g + 1) * rows, :tokens], values))

    spread(q_ref)
    q = q_wide[...]
    for j in range(2):
        for k in range(2):
            copy(r, j, k).wait()
    shown = lax.broadcasted_iota(jnp.int32, (positions, wide), 0) < lens[r] - me * positions
    s = jnp.where(shown, dot_nn(held[r, 0], q), NEGATIVE)
    step = lax.broadcasted_iota(jnp.int32, (fresh, wide), 1) % half // (half // STEPS)
    at = lax.broadcasted_iota(jnp.int32, (fresh, wide), 0)
    tail_shown = jnp.logical_and(at <= step, me == 0)
    t = jnp.where(tail_shown, dot_nn(tail_ref[0, 0], q), NEGATIVE)
    w, u = weigh(s, t, r)
    w = w.T
    u = jnp.concatenate([u, jnp.zeros((128 - fresh, wide), jnp.float32)], axis=0).T
    u = u.astype(jnp.bfloat16)
    for g in range(KVH):
        cols = slice(g * HD, (g + 1) * HD)
        mine = slice(g * rows, (g + 1) * rows)
        mean = dot_nn(w[mine, :], held[r, 1, :, cols])
        store(g, r, mean + dot_nn(u[mine, :fresh], tail_ref[1, 0, :, cols]))

    @pl.when(r == pl.num_programs(0) - 1)
    def _():
        x = lse_ref[...]
        high = x.astype(jnp.bfloat16).astype(jnp.float32)
        mid = (x - high).astype(jnp.bfloat16).astype(jnp.float32)
        low = x - high - mid
        rest = jnp.zeros((128 - 3 * x.shape[0], wide), jnp.float32)
        lines = jnp.concatenate([high, mid, low, rest], axis=0).T.astype(jnp.bfloat16)
        for d in range(TP):
            out_ref[d, 5] = lines[d * half : (d + 1) * half, :]


def partials(info, lengths, q, arrival, cache_kv, tail, pre_kv):
    requests = lengths.shape[0]
    positions = cache_kv.shape[2]
    tokens = pre_kv.shape[1]
    fresh = tail.shape[2]
    rows = q.shape[2]
    half = rows // 2
    return pl.pallas_call(
        partial_kernel,
        out_shape=jax.ShapeDtypeStruct((TP, requests + 2, half, HD), jnp.bfloat16),
        grid_spec=pltpu.PrefetchScalarGridSpec(
            num_scalar_prefetch=2,
            grid=(requests,),
            in_specs=[
                pl.BlockSpec((1, KVH, rows, HD), lambda r, *_: (r, 0, 0, 0)),
                pl.BlockSpec((1, KVH, rows, HD), lambda r, *_: (0, 0, 0, 0)),
                pl.BlockSpec(memory_space=pl.ANY),
                pl.BlockSpec((2, 1, fresh, KVH * HD), lambda r, *_: (0, r, 0, 0)),
                pl.BlockSpec((2, tokens, KVH * HD), lambda r, *_: (0, 0, 0)),
            ],
            out_specs=pl.BlockSpec((TP, requests + 2, half, HD), lambda r, *_: (0, 0, 0, 0)),
            scratch_shapes=[
                pltpu.VMEM((KVH * HD, KVH * rows), jnp.bfloat16),
                pltpu.VMEM((8, KVH * rows), jnp.float32),
                pltpu.VMEM((requests, 2, positions, KVH * HD), jnp.bfloat16),
                pltpu.SemaphoreType.DMA((requests, 2, 2)),
            ],
        ),
        compiler_params=params(),
        cost_estimate=pl.CostEstimate(
            flops=40 * rows * KVH * positions * HD * requests,
            bytes_accessed=4 * requests * positions * KVH * HD,
            transcendentals=rows * KVH * positions * requests,
        ),
        name="partials",
    )(info, lengths, q, arrival, cache_kv, tail, pre_kv)


def merge_kernel(x_ref, dec_ref, arr_ref):
    lse = x_ref[:, 5].astype(jnp.float32)
    lane = lax.broadcasted_iota(jnp.int32, lse.shape, 2)
    for slot in range(5):
        pick = jnp.logical_and(lane % 8 == slot, lane < 24)
        mine = jnp.sum(jnp.where(pick, lse, 0.0), axis=-1, keepdims=True)
        top = jnp.max(mine, axis=0, keepdims=True)
        w = jnp.exp2(mine - top)
        total = jnp.sum(w, axis=0)
        mixed = jnp.sum(w * x_ref[:, slot].astype(jnp.float32), axis=0) / total
        if slot < 4:
            dec_ref[slot] = mixed.astype(jnp.bfloat16)
        else:
            arr_ref[...] = mixed.astype(jnp.bfloat16)


def merge(x):
    half = x.shape[2]
    return pl.pallas_call(
        merge_kernel,
        out_shape=(
            jax.ShapeDtypeStruct((4, half, HD), jnp.bfloat16),
            jax.ShapeDtypeStruct((half, HD), jnp.bfloat16),
        ),
        name="merge",
    )(x)


def select_kernel(table, x_ref, arr_ref, out_ref):
    tokens = x_ref.shape[1]
    pool = table[2 * POOL * MOST]
    extra = arr_ref.shape[0]
    for d in range(POOL):
        for m in range(MOST):
            prompt = table[d * MOST + m]
            held = table[POOL * MOST + d * MOST + m] == 1
            x = x_ref[pl.ds(prompt, 1)]
            out_ref[d, m, :tokens] = jnp.where(held, x, jnp.zeros_like(x))[0]
            row = jnp.where(
                jnp.logical_and(held, prompt == pool), arr_ref[...], jnp.zeros_like(arr_ref)
            )
            out_ref[d, m, tokens:, :HD] = row
            out_ref[d, m, tokens:, HD:] = jnp.zeros((extra, x.shape[2] - HD), jnp.bfloat16)


def select(table, pieces, arrived):
    _, tokens, width = pieces.shape
    extra = arrived.shape[0]
    return pl.pallas_call(
        select_kernel,
        out_shape=jax.ShapeDtypeStruct((POOL, MOST, tokens + extra, width), jnp.bfloat16),
        in_specs=[
            pl.BlockSpec(memory_space=pltpu.SMEM),
            pl.BlockSpec(memory_space=pltpu.VMEM),
            pl.BlockSpec(memory_space=pltpu.VMEM),
        ],
        out_specs=pl.BlockSpec(memory_space=pltpu.VMEM),
        compiler_params=params(),
        name="select",
    )(table, pieces, arrived)


def settle_kernel(table, x_ref, kv_ref, arr_ref):
    tokens = kv_ref.shape[2]
    width = x_ref.shape[3]
    pool = table[2 * POOL * MOST]
    for m in range(MOST):
        for i in range(POOL):
            at = i % 4 * width
            kv_ref[i // 4, m, :, at : at + width] = x_ref[i, m, :tokens]
        prompt = table[pool * MOST + m]
        arr_ref[m] = x_ref[pl.ds(prompt, 1), m, tokens:, :HD][0]


def settle(table, x):
    _, _, rows, width = x.shape
    tokens = rows - 16
    return pl.pallas_call(
        settle_kernel,
        out_shape=(
            jax.ShapeDtypeStruct((2, MOST, tokens, KVH * HD), jnp.bfloat16),
            jax.ShapeDtypeStruct((MOST, rows - tokens, HD), jnp.bfloat16),
        ),
        in_specs=[
            pl.BlockSpec(memory_space=pltpu.SMEM),
            pl.BlockSpec(memory_space=pltpu.VMEM),
        ],
        out_specs=(
            pl.BlockSpec(memory_space=pltpu.VMEM),
            pl.BlockSpec(memory_space=pltpu.VMEM),
        ),
        compiler_params=params(),
        name="settle",
    )(table, x)


def body(pre_q, pre_kv, arrival_q, owner, cache_kv, lengths, dec_q, new_kv):
    tokens = pre_q.shape[0]
    me = lax.axis_index("tp").astype(jnp.int32)
    pool = lax.axis_index("pool").astype(jnp.int32)
    x, y = me // 4, me // 2 % 2
    flags = [x >= 1, x >= 2, x == 3, y == 1]
    info = jnp.stack([me, me % 2] + [f.astype(jnp.int32) for f in flags])
    back1, back2, wrapped, upper = 2, 3, 4, 5

    def permute(a, pairs):
        return lax.ppermute(a, "tp", pairs)

    swap = [(t, t ^ 1) for t in range(TP)]
    across = [(t, t ^ 2) for t in range(TP)]
    forward = [(t, t + 4) for t in range(12)]
    around = [(t, t + 12) for t in range(4)]

    at = np.arange(REP * tokens) % tokens
    sides = jnp.stack([me % 2, 1 - me % 2]) * tokens
    pos = (sides[:, None] + at[None]).astype(jnp.int32).reshape(2, -1, COLS)

    prompts = jnp.arange(owner.shape[0])
    earlier = jnp.logical_and(
        owner[:, None] == owner[None, :], prompts[None, :] < prompts[:, None]
    )
    rank = jnp.sum(earlier.astype(jnp.int32), axis=1)
    hit = jnp.logical_and(
        owner[None, None, :] == jnp.arange(POOL)[:, None, None],
        rank[None, None, :] == jnp.arange(MOST)[None, :, None],
    )
    held = jnp.any(hit, axis=-1).astype(jnp.int32)
    prompt_of = jnp.sum(hit.astype(jnp.int32) * prompts, axis=-1).astype(jnp.int32)
    table = jnp.concatenate([prompt_of.reshape(-1), held.reshape(-1), pool[None]])

    requests = lengths.shape[0]
    dec_rows = dec_q.reshape(STEPS, requests, KVH, 2, REP // 2, HD)
    dec_rows = jnp.transpose(dec_rows, (1, 2, 3, 0, 4, 5)).reshape(requests, KVH, STEPS * REP, HD)
    arrival = lax.dynamic_index_in_dim(arrival_q, pool, 0, False)
    arrival = arrival.reshape(KVH, 2, 1, REP // 2, HD)
    arrival = jnp.pad(arrival, ((0, 0), (0, 0), (0, STEPS - 1), (0, 0), (0, 0)))
    arrival = arrival.reshape(1, KVH, STEPS * REP, HD)
    tail = jnp.pad(jnp.transpose(new_kv, (0, 2, 1, 3)), ((0, 0), (0, 0), (0, 12), (0, 0)))

    kv_own, kv_send, pieces = prep_kv(info, pre_kv)
    kv_swapped = permute(kv_send, swap)
    q_send = other_half(info, pre_q)
    own = jnp.stack([kv_own, kv_swapped])
    own, q_send, info_decode = lax.optimization_barrier((own, q_send, info))

    a1 = permute(own, forward)
    b0 = permute(own, across)
    w1 = permute(own, around)
    q_sib = permute(q_send, swap)
    part = partials(info_decode, lengths, dec_rows, arrival, cache_kv, tail, pre_kv)
    part = lax.all_to_all(part, "tp", 0, 0)
    part, a1, b0, w1, own, q_sib, info = lax.optimization_barrier(
        (part, a1, b0, w1, own, q_sib, info)
    )

    def take(order, parts, kinds, carry, last):
        return prefill(order, pos, pre_q, q_sib, parts, kinds, carry, last)

    a2 = permute(a1, forward[4:])
    b1 = permute(a1, across[4:])
    w2 = permute(b0, around)
    part, pieces, info = lax.optimization_barrier((part, pieces, info))
    pieces = lax.all_to_all(pieces, "pool", 0, 0)
    carry = take(info, [own, a1, b0, w1], [-1, back1, upper, wrapped], None, False)
    part, pieces, carry, a2, b1, w2, info = lax.optimization_barrier(
        (part, pieces, carry, a2, b1, w2, info)
    )
    decoded, arrived = merge(part)

    b2 = permute(b1, forward[4:])
    landed = lax.all_to_all(select(table, pieces, arrived), "pool", 0, 0)
    carry = take(info, [a2, b1, w2], [back2, back1, wrapped], carry, False)
    carry, b2, landed, info = lax.optimization_barrier((carry, b2, landed, info))

    out, out_send = take(info, [b2], [back2], carry, True)
    received, arrival_rows = settle(table, landed)
    prefill_out = place(info, out, permute(out_send, swap))
    arrival_out = arrival_rows[:, : REP // 2].reshape(MOST, REP // 2 * HD)
    decode_out = jnp.transpose(
        decoded.reshape(requests, STEPS, REP // 2, HD), (1, 0, 2, 3)
    ).reshape(STEPS, requests, REP // 2 * HD)
    return (prefill_out, received, decode_out, arrival_out)


def solution(mesh):
    in_specs = (
        P(("pool", "tp"), None),
        P(None, ("pool", "tp"), None),
        P(),
        P(),
        P(None, "pool", "tp", None),
        P("pool"),
        P(None, "pool", None),
        P(None, None, "pool", None),
    )
    out_specs = (
        P(("pool", "tp"), None),
        P(None, "pool", "tp", None),
        P(None, "pool", "tp"),
        P("pool", "tp"),
    )
    return jax.shard_map(body, mesh=mesh, in_specs=in_specs, out_specs=out_specs, check_vma=False)
```

```python
import functools
import math

import jax
import jax.numpy as jnp
import numpy as np
from jax import lax
from jax.experimental import pallas as pl
from jax.experimental.pallas import tpu as pltpu
from jax.sharding import PartitionSpec as P

H = 64
KVH = 8
REP = H // KVH
HD = 128
STEPS = 4
MOST = 2
POOL = 8
TP = 16
HALF = KVH // 2
NEGATIVE = -1e30
FLOOR = -1e29
SCALE2 = math.log2(math.e) / math.sqrt(HD)
LOG2E = math.log2(math.e)
TILE = 256
UNIT = 64
COLS = 256
VMEM_BYTES = 48 * 1024 * 1024


def params(limit=VMEM_BYTES):
    return pltpu.CompilerParams(vmem_limit_bytes=limit)


def dot_nt(a, b):
    return lax.dot_general(a, b, (((1,), (1,)), ((), ())), preferred_element_type=jnp.float32)


def dot_nn(a, b):
    return lax.dot_general(a, b, (((1,), (0,)), ((), ())), preferred_element_type=jnp.float32)


def prep_kv_kernel(info, kv_ref, own_ref, sib_ref, piece_ref):
    core = info[1]
    for g in range(HALF):
        for half, ref in ((core, own_ref), (1 - core, sib_ref)):
            at = pl.multiple_of((half * HALF + g) * HD, HD)
            ref[g] = kv_ref[:, :, pl.ds(at, HD)]
    width = piece_ref.shape[2]
    for i in range(POOL):
        at = i % 4 * width
        piece_ref[i] = kv_ref[i // 4, :, at : at + width]


def prep_kv(info, pre_kv):
    _, tokens, width = pre_kv.shape
    half = jax.ShapeDtypeStruct((HALF, 2, tokens, HD), jnp.bfloat16)
    return pl.pallas_call(
        prep_kv_kernel,
        out_shape=(half, half, jax.ShapeDtypeStruct((POOL, tokens, width // 4), jnp.bfloat16)),
        grid_spec=pltpu.PrefetchScalarGridSpec(
            num_scalar_prefetch=1,
            grid=(1,),
            in_specs=[pl.BlockSpec((2, tokens, width), lambda i, s: (0, 0, 0))],
            out_specs=(
                pl.BlockSpec((HALF, 2, tokens, HD), lambda i, s: (0, 0, 0, 0)),
                pl.BlockSpec((HALF, 2, tokens, HD), lambda i, s: (0, 0, 0, 0)),
                pl.BlockSpec((POOL, tokens, width // 4), lambda i, s: (0, 0, 0)),
            ),
        ),
        compiler_params=params(),
        name="prep_kv",
    )(info, pre_kv)


def copy_kernel(info, x_ref, out_ref):
    out_ref[...] = x_ref[...]


def other_half(info, pre_q):
    tokens = pre_q.shape[0]
    return pl.pallas_call(
        copy_kernel,
        out_shape=jax.ShapeDtypeStruct((tokens, HALF * REP * HD), jnp.bfloat16),
        grid_spec=pltpu.PrefetchScalarGridSpec(
            num_scalar_prefetch=1,
            grid=(2,),
            in_specs=[
                pl.BlockSpec((tokens, 2 * REP * HD), lambda g, s: (0, (1 - s[1]) * 2 + g))
            ],
            out_specs=pl.BlockSpec((tokens, 2 * REP * HD), lambda g, s: (0, g)),
        ),
        compiler_params=params(),
        name="other_half",
    )(info, pre_q)


def place_kernel(info, kept_ref, x_ref, out_ref):
    del kept_ref
    out_ref[...] = x_ref[...]


def place(info, out, x):
    tokens, width = x.shape
    return pl.pallas_call(
        place_kernel,
        out_shape=jax.ShapeDtypeStruct(out.shape, out.dtype),
        grid_spec=pltpu.PrefetchScalarGridSpec(
            num_scalar_prefetch=1,
            grid=(5,),
            in_specs=[
                pl.BlockSpec(memory_space=pl.ANY),
                pl.BlockSpec((tokens // 5, width), lambda i, s: (i, 0)),
            ],
            out_specs=pl.BlockSpec((tokens // 5, width), lambda i, s: (i, 1 - s[1])),
        ),
        input_output_aliases={1: 0},
        compiler_params=params(),
        name="place",
    )(info, out, x)


def prefill_kernel(info, pos_ref, qa_ref, qb_ref, *refs, kinds, first, last):
    count = len(kinds)
    parts, refs = refs[:count], refs[count:]
    if not first:
        carry, refs = ((refs[0], refs[1]), (refs[2], refs[3])), refs[4:]
    if last:
        outs, refs = refs[:2], refs[2:]
    else:
        outs, refs = ((refs[0], refs[1]), (refs[2], refs[3])), refs[4:]
    k_all, v_all, v_across, q_all, s_all, top_all = refs[:6]
    g = pl.program_id(0)
    heads = pl.num_programs(0) - 1
    core = info[1]
    tokens = parts[0].shape[3]
    shard = 2 * tokens
    keys = count * shard
    blocks = q_all.shape[1] // COLS
    tiles = [(lo, min(lo + TILE, keys)) for lo in range(0, keys, TILE)]
    valid = [None if kind < 0 else info[kind] == 1 for kind in kinds]

    def load():
        for h in range(REP):
            at = h * tokens
            q_all[0, at : at + tokens, :] = qa_ref[:, h * HD : (h + 1) * HD]
            q_all[1, at : at + tokens, :] = qb_ref[:, h * HD : (h + 1) * HD]
        for i, part in enumerate(parts):
            for k in range(2):
                at = i * shard + k * tokens
                k_all[at : at + tokens, :] = part[k, 0, 0]
                v_all[at : at + tokens, :] = part[k, 0, 1]
        if v_all.shape[0] > keys:
            v_all[keys:, :] = jnp.zeros((v_all.shape[0] - keys, HD), jnp.bfloat16)
        for at in range(0, v_all.shape[0], 128):
            v_across[g % 2, :, at : at + 128] = v_all[at : at + 128, :].T

    def scores(side, n):
        q = q_all[side, n * COLS : (n + 1) * COLS, :]
        top = None
        for lo, hi in tiles:
            s = dot_nt(k_all[lo:hi, :], q)
            for at in range(lo, hi, UNIT):
                piece = s[at - lo : at - lo + UNIT, :]
                which = at // shard
                if valid[which] is None:
                    key = lax.broadcasted_iota(jnp.int32, piece.shape, 0) + (at - which * shard)
                    key = jnp.where(key < tokens, key + core * tokens, key - core * tokens)
                    seen = key <= pos_ref[side, n : n + 1, :]
                    piece = jnp.where(seen, piece, NEGATIVE)
                s_all[side, n, at : at + UNIT, :] = piece
                part = jnp.max(piece.reshape(UNIT // 8, 8, COLS), axis=0)
                if valid[which] is not None:
                    part = jnp.where(valid[which], part, NEGATIVE)
                top = part if top is None else jnp.maximum(top, part)
            yield
        top_all[side, n] = top

    def finish(side, n, slot):
        peak = jnp.max(top_all[side, n], axis=0, keepdims=True)
        if not first:
            acc_in, stat_in = carry[side]
            before = stat_in[0, n, 0:1, :]
            peak = jnp.maximum(before, peak)
            shrink = jnp.exp2((before - peak) * SCALE2)
        total = None
        acc = None
        for lo, hi in tiles:
            rounded = []
            for at in range(lo, hi, UNIT):
                which = at // shard
                base = peak if valid[which] is None else jnp.where(valid[which], peak, -NEGATIVE)
                w = jnp.exp2((s_all[side, n, at : at + UNIT, :] - base) * SCALE2)
                part = jnp.sum(w.reshape(UNIT // 8, 8, COLS), axis=0)
                total = part if total is None else total + part
                rounded.append(w.astype(jnp.bfloat16))
            w = jnp.concatenate(rounded, axis=0)
            part = dot_nn(v_across[slot, :, lo:hi], w)
            acc = part if acc is None else acc + part
            yield
        total = jnp.sum(total, axis=0, keepdims=True)
        if not first:
            acc = acc + acc_in[0, n].astype(jnp.float32) * shrink
            total = total + stat_in[0, n, 1:2, :] * shrink
        if last:
            stage = refs[6]
            stage[side, n * COLS : (n + 1) * COLS, :] = (acc * (1.0 / total)).T.astype(jnp.bfloat16)
        else:
            acc_out, stat_out = outs[side]
            acc_out[0, n] = acc.astype(jnp.bfloat16)
            line = lax.broadcasted_iota(jnp.int32, (8, COLS), 0)
            stat_out[0, n] = jnp.where(line == 0, peak, total)

    def drain(steps):
        live = list(steps)
        while live:
            for step in list(live):
                if next(step, live) is live:
                    live.remove(step)

    def both(scored, finished, slot):
        if scored == 0:
            load()
        for n in range(blocks):
            steps = [] if scored is None else [scores(scored, n)]
            if finished is not None:
                steps.append(finish(finished, n, slot))
            drain(steps)
        if last and finished is not None:
            stage = refs[6]
            for h in range(REP):
                at = h * tokens
                outs[finished][:, h * HD : (h + 1) * HD] = stage[finished, at : at + tokens, :]

    before = (g + 1) % 2
    pl.when(g == 0)(lambda: both(0, None, None))
    pl.when(jnp.logical_and(g > 0, g < heads))(lambda: both(0, 1, before))
    pl.when(g == heads)(lambda: both(None, 1, before))
    pl.when(g < heads)(lambda: both(1, 0, g % 2))


def prefill(info, pos, pre_q, q_sib, parts, kinds, carry, last):
    tokens = pre_q.shape[0]
    rows = REP * tokens
    blocks = rows // COLS
    first = carry is None
    keys = len(parts) * 2 * tokens
    room = -(-keys // 128) * 128

    def now(g):
        return jnp.minimum(g, HALF - 1)

    def late(g):
        return jnp.maximum(g - 1, 0)

    in_specs = [
        pl.BlockSpec(pos.shape, lambda g, s: (0, 0, 0)),
        pl.BlockSpec((tokens, REP * HD), lambda g, s: (0, s[1] * HALF + now(g))),
        pl.BlockSpec((tokens, REP * HD), lambda g, s: (0, now(g))),
    ]
    in_specs += [
        pl.BlockSpec((2, 1, 2, tokens, HD), lambda g, s: (0, now(g), 0, 0, 0)) for _ in parts
    ]
    args = [pos, pre_q, q_sib, *parts]
    carry_specs = [
        pl.BlockSpec((1, blocks, HD, COLS), lambda g, s: (now(g), 0, 0, 0)),
        pl.BlockSpec((1, blocks, 8, COLS), lambda g, s: (now(g), 0, 0, 0)),
        pl.BlockSpec((1, blocks, HD, COLS), lambda g, s: (late(g), 0, 0, 0)),
        pl.BlockSpec((1, blocks, 8, COLS), lambda g, s: (late(g), 0, 0, 0)),
    ]
    if not first:
        in_specs += carry_specs
        args += list(carry)
    scratch = [
        pltpu.VMEM((keys, HD), jnp.bfloat16),
        pltpu.VMEM((room, HD), jnp.bfloat16),
        pltpu.VMEM((2, HD, room), jnp.bfloat16),
        pltpu.VMEM((2, rows, HD), jnp.bfloat16),
        pltpu.VMEM((2, blocks, keys, COLS), jnp.float32),
        pltpu.VMEM((2, blocks, 8, COLS), jnp.float32),
    ]
    if last:
        out_shape = [
            jax.ShapeDtypeStruct(pre_q.shape, jnp.bfloat16),
            jax.ShapeDtypeStruct(q_sib.shape, jnp.bfloat16),
        ]
        out_specs = [
            pl.BlockSpec((tokens, REP * HD), lambda g, s: (0, s[1] * HALF + now(g))),
            pl.BlockSpec((tokens, REP * HD), lambda g, s: (0, late(g))),
        ]
        scratch.append(pltpu.VMEM((2, rows, HD), jnp.bfloat16))
    else:
        out_shape = [
            jax.ShapeDtypeStruct((HALF, blocks, HD, COLS), jnp.bfloat16),
            jax.ShapeDtypeStruct((HALF, blocks, 8, COLS), jnp.float32),
        ] * 2
        out_specs = carry_specs
    return pl.pallas_call(
        functools.partial(prefill_kernel, kinds=kinds, first=first, last=last),
        out_shape=out_shape,
        grid_spec=pltpu.PrefetchScalarGridSpec(
            num_scalar_prefetch=1,
            grid=(HALF + 1,),
            in_specs=in_specs,
            out_specs=out_specs,
            scratch_shapes=scratch,
        ),
        compiler_params=params(60 * 1024 * 1024),
        cost_estimate=pl.CostEstimate(
            flops=16 * HALF * rows * keys * HD,
            bytes_accessed=24 * HALF * rows * HD,
            transcendentals=2 * HALF * rows * keys,
        ),
        name="prefill",
    )(info, *args)


def partial_kernel(
    info, lens, q_ref, aq_ref, cache, tail_ref, pre_ref, out_ref, q_wide, lse_ref, held, sems
):
    me = info[0]
    r = pl.program_id(0)
    requests, _, positions, _ = held.shape
    fresh = tail_ref.shape[2]
    rows = q_ref.shape[2]
    wide = KVH * rows
    half = rows // 2

    chunk = positions // 2

    def copy(i, j, k):
        some = pl.ds(k * chunk, chunk)
        return pltpu.make_async_copy(
            cache.at[j, i, some], held.at[i, j, some], sems.at[i, j, k]
        )

    @pl.when(r == 0)
    def _():
        for i in range(requests):
            for j in range(2):
                for k in range(2):
                    copy(i, j, k).start()
        q_wide[...] = jnp.zeros_like(q_wide)
        lse_ref[...] = jnp.zeros_like(lse_ref)

    def spread(ref):
        lane = lax.broadcasted_iota(jnp.int32, (HD, 128), 1) // rows
        per = 128 // rows
        for i in range(KVH // per):
            turned = ref[0, i * per : (i + 1) * per].reshape(128, HD).T
            for j in range(per):
                g = i * per + j
                q_wide[g * HD : (g + 1) * HD, i * 128 : (i + 1) * 128] = jnp.where(
                    lane == j, turned, jnp.zeros_like(turned)
                )

    def fold(w):
        return w.reshape(w.shape[0] // 8, 8, wide)

    def weigh(s, t, slot):
        peak = jnp.max(jnp.max(fold(s), axis=0), axis=0, keepdims=True)
        if t is not None:
            peak = jnp.maximum(peak, jnp.max(t, axis=0, keepdims=True))
            peak = jnp.maximum(peak, FLOOR)
        s = jnp.exp2((s - peak) * SCALE2)
        total = jnp.sum(jnp.sum(fold(s), axis=0), axis=0, keepdims=True)
        if t is not None:
            t = jnp.exp2((t - peak) * SCALE2)
            total = total + jnp.sum(t, axis=0, keepdims=True)
        live = total > 0.0
        safe = jnp.where(live, total, 1.0)
        lse_ref[pl.ds(slot, 1), :] = jnp.where(
            live, peak * SCALE2 + jnp.log(safe) * LOG2E, NEGATIVE
        )
        share = jnp.where(live, 1.0 / safe, 0.0)
        s = (s * share).astype(jnp.bfloat16)
        return s, None if t is None else t * share

    def store(g, slot, mean):
        mean = mean.astype(jnp.bfloat16)
        for k in range(2):
            out_ref[2 * g + k, pl.ds(slot, 1)] = mean[k * half : (k + 1) * half][None]

    @pl.when(r == 0)
    def _():
        spread(aq_ref)
        tokens = pre_ref.shape[1]
        w, _ = weigh(dot_nn(pre_ref[0], q_wide[...]), None, 4)
        w = jnp.concatenate([w, jnp.zeros((256 - tokens, wide), jnp.bfloat16)], axis=0).T
        for g in range(KVH):
            values = pre_ref[1, :, g * HD : (g + 1) * HD]
            store(g, 4, dot_nn(w[g * rows : (g + 1) * rows, :tokens], values))

    spread(q_ref)
    q = q_wide[...]
    for j in range(2):
        for k in range(2):
            copy(r, j, k).wait()
    shown = lax.broadcasted_iota(jnp.int32, (positions, wide), 0) < lens[r] - me * positions
    s = jnp.where(shown, dot_nn(held[r, 0], q), NEGATIVE)
    step = lax.broadcasted_iota(jnp.int32, (fresh, wide), 1) % half // (half // STEPS)
    at = lax.broadcasted_iota(jnp.int32, (fresh, wide), 0)
    tail_shown = jnp.logical_and(at <= step, me == 0)
    t = jnp.where(tail_shown, dot_nn(tail_ref[0, 0], q), NEGATIVE)
    w, u = weigh(s, t, r)
    w = w.T
    u = jnp.concatenate([u, jnp.zeros((128 - fresh, wide), jnp.float32)], axis=0).T
    u = u.astype(jnp.bfloat16)
    for g in range(KVH):
        cols = slice(g * HD, (g + 1) * HD)
        mine = slice(g * rows, (g + 1) * rows)
        mean = dot_nn(w[mine, :], held[r, 1, :, cols])
        store(g, r, mean + dot_nn(u[mine, :fresh], tail_ref[1, 0, :, cols]))

    @pl.when(r == pl.num_programs(0) - 1)
    def _():
        x = lse_ref[...]
        high = x.astype(jnp.bfloat16).astype(jnp.float32)
        mid = (x - high).astype(jnp.bfloat16).astype(jnp.float32)
        low = x - high - mid
        rest = jnp.zeros((128 - 3 * x.shape[0], wide), jnp.float32)
        lines = jnp.concatenate([high, mid, low, rest], axis=0).T.astype(jnp.bfloat16)
        for d in range(TP):
            out_ref[d, 5] = lines[d * half : (d + 1) * half, :]


def partials(info, lengths, q, arrival, cache_kv, tail, pre_kv):
    requests = lengths.shape[0]
    positions = cache_kv.shape[2]
    tokens = pre_kv.shape[1]
    fresh = tail.shape[2]
    rows = q.shape[2]
    half = rows // 2
    return pl.pallas_call(
        partial_kernel,
        out_shape=jax.ShapeDtypeStruct((TP, requests + 2, half, HD), jnp.bfloat16),
        grid_spec=pltpu.PrefetchScalarGridSpec(
            num_scalar_prefetch=2,
            grid=(requests,),
            in_specs=[
                pl.BlockSpec((1, KVH, rows, HD), lambda r, *_: (r, 0, 0, 0)),
                pl.BlockSpec((1, KVH, rows, HD), lambda r, *_: (0, 0, 0, 0)),
                pl.BlockSpec(memory_space=pl.ANY),
                pl.BlockSpec((2, 1, fresh, KVH * HD), lambda r, *_: (0, r, 0, 0)),
                pl.BlockSpec((2, tokens, KVH * HD), lambda r, *_: (0, 0, 0)),
            ],
            out_specs=pl.BlockSpec((TP, requests + 2, half, HD), lambda r, *_: (0, 0, 0, 0)),
            scratch_shapes=[
                pltpu.VMEM((KVH * HD, KVH * rows), jnp.bfloat16),
                pltpu.VMEM((8, KVH * rows), jnp.float32),
                pltpu.VMEM((requests, 2, positions, KVH * HD), jnp.bfloat16),
                pltpu.SemaphoreType.DMA((requests, 2, 2)),
            ],
        ),
        compiler_params=params(),
        cost_estimate=pl.CostEstimate(
            flops=40 * rows * KVH * positions * HD * requests,
            bytes_accessed=4 * requests * positions * KVH * HD,
            transcendentals=rows * KVH * positions * requests,
        ),
        name="partials",
    )(info, lengths, q, arrival, cache_kv, tail, pre_kv)


def merge_kernel(x_ref, dec_ref, arr_ref):
    lse = x_ref[:, 5].astype(jnp.float32)
    lane = lax.broadcasted_iota(jnp.int32, lse.shape, 2)
    for slot in range(5):
        pick = jnp.logical_and(lane % 8 == slot, lane < 24)
        mine = jnp.sum(jnp.where(pick, lse, 0.0), axis=-1, keepdims=True)
        top = jnp.max(mine, axis=0, keepdims=True)
        w = jnp.exp2(mine - top)
        total = jnp.sum(w, axis=0)
        mixed = jnp.sum(w * x_ref[:, slot].astype(jnp.float32), axis=0) / total
        if slot < 4:
            dec_ref[slot] = mixed.astype(jnp.bfloat16)
        else:
            arr_ref[...] = mixed.astype(jnp.bfloat16)


def merge(x):
    half = x.shape[2]
    return pl.pallas_call(
        merge_kernel,
        out_shape=(
            jax.ShapeDtypeStruct((4, half, HD), jnp.bfloat16),
            jax.ShapeDtypeStruct((half, HD), jnp.bfloat16),
        ),
        name="merge",
    )(x)


def select_kernel(table, x_ref, arr_ref, out_ref):
    tokens = x_ref.shape[1]
    pool = table[2 * POOL * MOST]
    extra = arr_ref.shape[0]
    for d in range(POOL):
        for m in range(MOST):
            prompt = table[d * MOST + m]
            held = table[POOL * MOST + d * MOST + m] == 1
            x = x_ref[pl.ds(prompt, 1)]
            out_ref[d, m, :tokens] = jnp.where(held, x, jnp.zeros_like(x))[0]
            row = jnp.where(
                jnp.logical_and(held, prompt == pool), arr_ref[...], jnp.zeros_like(arr_ref)
            )
            out_ref[d, m, tokens:, :HD] = row
            out_ref[d, m, tokens:, HD:] = jnp.zeros((extra, x.shape[2] - HD), jnp.bfloat16)


def select(table, pieces, arrived):
    _, tokens, width = pieces.shape
    extra = arrived.shape[0]
    return pl.pallas_call(
        select_kernel,
        out_shape=jax.ShapeDtypeStruct((POOL, MOST, tokens + extra, width), jnp.bfloat16),
        in_specs=[
            pl.BlockSpec(memory_space=pltpu.SMEM),
            pl.BlockSpec(memory_space=pltpu.VMEM),
            pl.BlockSpec(memory_space=pltpu.VMEM),
        ],
        out_specs=pl.BlockSpec(memory_space=pltpu.VMEM),
        compiler_params=params(),
        name="select",
    )(table, pieces, arrived)


def settle_kernel(table, x_ref, kv_ref, arr_ref):
    tokens = kv_ref.shape[2]
    width = x_ref.shape[3]
    pool = table[2 * POOL * MOST]
    for m in range(MOST):
        for i in range(POOL):
            at = i % 4 * width
            kv_ref[i // 4, m, :, at : at + width] = x_ref[i, m, :tokens]
        prompt = table[pool * MOST + m]
        arr_ref[m] = x_ref[pl.ds(prompt, 1), m, tokens:, :HD][0]


def settle(table, x):
    _, _, rows, width = x.shape
    tokens = rows - 16
    return pl.pallas_call(
        settle_kernel,
        out_shape=(
            jax.ShapeDtypeStruct((2, MOST, tokens, KVH * HD), jnp.bfloat16),
            jax.ShapeDtypeStruct((MOST, rows - tokens, HD), jnp.bfloat16),
        ),
        in_specs=[
            pl.BlockSpec(memory_space=pltpu.SMEM),
            pl.BlockSpec(memory_space=pltpu.VMEM),
        ],
        out_specs=(
            pl.BlockSpec(memory_space=pltpu.VMEM),
            pl.BlockSpec(memory_space=pltpu.VMEM),
        ),
        compiler_params=params(),
        name="settle",
    )(table, x)


def body(pre_q, pre_kv, arrival_q, owner, cache_kv, lengths, dec_q, new_kv):
    tokens = pre_q.shape[0]
    me = lax.axis_index("tp").astype(jnp.int32)
    pool = lax.axis_index("pool").astype(jnp.int32)
    x, y = me // 4, me // 2 % 2
    flags = [x >= 1, x >= 2, x == 3, y == 1]
    info = jnp.stack([me, me % 2] + [f.astype(jnp.int32) for f in flags])
    back1, back2, wrapped, upper = 2, 3, 4, 5

    def permute(a, pairs):
        return lax.ppermute(a, "tp", pairs)

    swap = [(t, t ^ 1) for t in range(TP)]
    across = [(t, t ^ 2) for t in range(TP)]
    forward = [(t, t + 4) for t in range(12)]
    around = [(t, t + 12) for t in range(4)]

    at = np.arange(REP * tokens) % tokens
    sides = jnp.stack([me % 2, 1 - me % 2]) * tokens
    pos = (sides[:, None] + at[None]).astype(jnp.int32).reshape(2, -1, COLS)

    prompts = jnp.arange(owner.shape[0])
    earlier = jnp.logical_and(
        owner[:, None] == owner[None, :], prompts[None, :] < prompts[:, None]
    )
    rank = jnp.sum(earlier.astype(jnp.int32), axis=1)
    hit = jnp.logical_and(
        owner[None, None, :] == jnp.arange(POOL)[:, None, None],
        rank[None, None, :] == jnp.arange(MOST)[None, :, None],
    )
    held = jnp.any(hit, axis=-1).astype(jnp.int32)
    prompt_of = jnp.sum(hit.astype(jnp.int32) * prompts, axis=-1).astype(jnp.int32)
    table = jnp.concatenate([prompt_of.reshape(-1), held.reshape(-1), pool[None]])

    requests = lengths.shape[0]
    dec_rows = dec_q.reshape(STEPS, requests, KVH, 2, REP // 2, HD)
    dec_rows = jnp.transpose(dec_rows, (1, 2, 3, 0, 4, 5)).reshape(requests, KVH, STEPS * REP, HD)
    arrival = lax.dynamic_index_in_dim(arrival_q, pool, 0, False)
    arrival = arrival.reshape(KVH, 2, 1, REP // 2, HD)
    arrival = jnp.pad(arrival, ((0, 0), (0, 0), (0, STEPS - 1), (0, 0), (0, 0)))
    arrival = arrival.reshape(1, KVH, STEPS * REP, HD)
    tail = jnp.pad(jnp.transpose(new_kv, (0, 2, 1, 3)), ((0, 0), (0, 0), (0, 12), (0, 0)))

    kv_own, kv_send, pieces = prep_kv(info, pre_kv)
    kv_swapped = permute(kv_send, swap)
    q_send = other_half(info, pre_q)
    own = jnp.stack([kv_own, kv_swapped])
    own, q_send, info_decode = lax.optimization_barrier((own, q_send, info))

    a1 = permute(own, forward)
    b0 = permute(own, across)
    w1 = permute(own, around)
    q_sib = permute(q_send, swap)
    part = partials(info_decode, lengths, dec_rows, arrival, cache_kv, tail, pre_kv)
    part = lax.all_to_all(part, "tp", 0, 0)
    part, a1, b0, w1, own, q_sib, info = lax.optimization_barrier(
        (part, a1, b0, w1, own, q_sib, info)
    )

    def take(order, parts, kinds, carry, last):
        return prefill(order, pos, pre_q, q_sib, parts, kinds, carry, last)

    a2 = permute(a1, forward[4:])
    b1 = permute(a1, across[4:])
    w2 = permute(b0, around)
    part, pieces, info = lax.optimization_barrier((part, pieces, info))
    pieces = lax.all_to_all(pieces, "pool", 0, 0)
    carry = take(info, [own, a1, b0, w1], [-1, back1, upper, wrapped], None, False)
    part, pieces, carry, a2, b1, w2, info = lax.optimization_barrier(
        (part, pieces, carry, a2, b1, w2, info)
    )
    decoded, arrived = merge(part)

    b2 = permute(b1, forward[4:])
    landed = lax.all_to_all(select(table, pieces, arrived), "pool", 0, 0)
    carry = take(info, [a2, b1, w2], [back2, back1, wrapped], carry, False)
    carry, b2, landed, info = lax.optimization_barrier((carry, b2, landed, info))

    out, out_send = take(info, [b2], [back2], carry, True)
    received, arrival_rows = settle(table, landed)
    prefill_out = place(info, out, permute(out_send, swap))
    arrival_out = arrival_rows[:, : REP // 2].reshape(MOST, REP // 2 * HD)
    decode_out = jnp.transpose(
        decoded.reshape(requests, STEPS, REP // 2, HD), (1, 0, 2, 3)
    ).reshape(STEPS, requests, REP // 2 * HD)
    return (prefill_out, received, decode_out, arrival_out)


def solution(mesh):
    in_specs = (
        P(("pool", "tp"), None),
        P(None, ("pool", "tp"), None),
        P(),
        P(),
        P(None, "pool", "tp", None),
        P("pool"),
        P(None, "pool", None),
        P(None, None, "pool", None),
    )
    out_specs = (
        P(("pool", "tp"), None),
        P(None, "pool", "tp", None),
        P(None, "pool", "tp"),
        P("pool", "tp"),
    )
    return jax.shard_map(body, mesh=mesh, in_specs=in_specs, out_specs=out_specs, check_vma=False)
```
